32 devices in a mesh: mgroup: 8 (over z, core), msub: 4 (over y, x).
Axes of the slice: x: 2, y: 2, z: 4, core: 2. Of those that a mesh axis runs over, the one named last changes fastest.
Arguments:
- in_modes: int32 [32, 2], P(('mgroup', 'msub')), may hold values from 0 to 31
- back_first: bfloat16 [32, 1024, 2048], P(('mgroup', 'msub')), may hold values from -48 to 48
- back_second: bfloat16 [32, 1024, 2048], P(('mgroup', 'msub')), may hold values from -144 to 144
Outputs:
- mask_first: float32 [1024, 2048], P(('mgroup', 'msub'))
- mask_second: float32 [1024, 2048], P(('mgroup', 'msub'))
The draws below stay inside these ranges and needn't reach their ends.
Inputs may be any that keep to these rules, and one draw needn't show every extreme that they name: `in_modes`: each row holds a mode's row order and column order.
All inputs are finite; a program needn't handle non-finite values.
Results may differ from the reference program's by a relative error of at most 0.013.
Values may be sent and summed in bfloat16 or wider, within the bound.
A program may use at most 128 MiB of HBM per device.

```python
import math
import jax
import jax.numpy as jnp
from jax import lax

G = 1024
ORDERS = 32
MODES = 32


def set_ends(result, own_key, least, largest):
    longest = result.shape.index(max(result.shape))
    spots = []
    for shift in (0, 1):
        where = [jax.random.randint(jax.random.fold_in(own_key, axis), (), 0, length) for axis, length in enumerate(result.shape)]
        where[longest] = (where[longest] + shift) % result.shape[longest]
        spots.append(tuple(where))
    return result.at[spots[0]].set(least).at[spots[1]].set(largest)


def strengthened(drawn, key, source, target, shards_of, factor):
    def block_of(axis_at):
        return (jnp.arange(drawn.shape[axis_at]) // (drawn.shape[axis_at] // shards_of)).reshape((-1,) + (1,) * (drawn.ndim - 1 - axis_at))

    one_side = jax.random.permutation(key, shards_of)[block_of(target)]
    second = (block_of(target) + shards_of // 2) % shards_of
    return jnp.where((block_of(source) == one_side) | (block_of(source) == second), factor * drawn, drawn)


def block_scale(key, dims, pieces, low, largest):
    level = 1.0
    for dim, blocks in pieces:
        heights = jax.random.uniform(jax.random.fold_in(jax.random.fold_in(key, 6), dim), (blocks,), jnp.float32, low / len(pieces), largest / len(pieces))
        level = level * jnp.repeat(jnp.exp(heights), dims[dim] // blocks).reshape((-1,) + (1,) * (len(dims) - 1 - dim))
    return level


def heavy_noise(own_key, shape, scale, reach, shards, heavy, kind=jnp.bfloat16):
    array = scale * jax.random.normal(own_key, shape, jnp.float32)
    if shards:
        array = array * block_scale(own_key, shape, shards, -0.22, 0.18)
    return jnp.clip(strengthened(array, jax.random.fold_in(own_key, 3), *heavy), -reach, reach).astype(kind)


def setup_inputs(seed: int = 0) -> dict:
    key_list = jax.random.split(jax.random.key(seed), 4)
    in_modes = set_ends(jax.random.randint(key_list[0], (MODES, 2), 0, ORDERS), jax.random.fold_in(key_list[0], 1), 0, ORDERS - 1).astype(jnp.int32)
    back_first = heavy_noise(key_list[1], (MODES, G, 2 * G), 8.0, 48.0, ((0, 32),), (0, 1, 32, 2.75))
    back_second = heavy_noise(key_list[2], (MODES, G, 2 * G), 24.0, 144.0, ((0, 32),), (0, 1, 32, 2.75))
    return dict(in_modes=in_modes, back_first=back_first, back_second=back_second)


span_width = 24.0

def grid_points(cells):
    index = jnp.arange(cells, dtype=jnp.float32)
    return (index - cells / 2 + 0.5) * (span_width / cells)

def hermite_table(points):
    before = jnp.zeros_like(points)
    current = math.pi ** (-0.25) * jnp.exp(-0.5 * points * points)
    collected = []
    for order in range(ORDERS):
        collected.append(current)
        following = math.sqrt(2.0 / (order + 1)) * points * current - math.sqrt(order / (order + 1.0)) * before
        before, current = (current, following)
    return jnp.stack(collected, axis=0)

def chirp_parts(cells):
    index = jnp.arange(cells, dtype=jnp.int32)
    offset = index[:, None] - index[None, :]
    square = offset * offset % (2 * cells)
    phase = square.astype(jnp.float32) * (math.pi / cells)
    factor = cells ** (-0.5)
    return ((jnp.cos(phase) * factor).astype(jnp.bfloat16), (jnp.sin(phase) * factor).astype(jnp.bfloat16))

def soften(intersection):
    half = intersection.shape[-1] // 2
    real_part = intersection[..., :half]
    imag_part = intersection[..., half:]
    denom = jnp.sqrt(real_part * real_part + imag_part * imag_part + 1.0)
    return intersection / jnp.concatenate([denom, denom], axis=-1)

def reference(in_modes, back_first, back_second):
    cells = G
    herm_table = hermite_table(grid_points(cells))
    row_funcs = herm_table[in_modes[:, 0]]
    col_funcs = herm_table[in_modes[:, 1]]
    chirp_real, chirp_imag = chirp_parts(cells)
    big_chirp = jnp.concatenate([jnp.concatenate([chirp_real, chirp_imag], axis=1), jnp.concatenate([-chirp_imag, chirp_real], axis=1)], axis=0)
    scale_all = float(MODES) ** (-0.5)

    def first_term(running, mode_item):
        row_one, col_one, back_one = mode_item
        fields = (row_one[:, None] * col_one[None, :]).astype(jnp.bfloat16).astype(jnp.float32)
        tiled = jnp.concatenate([fields, fields], axis=1)
        return (running + back_one.astype(jnp.float32) * tiled, None)
    intersection_one, _ = lax.scan(first_term, jnp.zeros((cells, 2 * cells), jnp.float32), (row_funcs, col_funcs, back_first))
    mask_first = soften(intersection_one * scale_all)
    mask_low = mask_first.astype(jnp.bfloat16).astype(jnp.float32)

    def second_term(running, mode_item):
        row_one, col_one, back_one = mode_item
        fields = (row_one[:, None] * col_one[None, :]).astype(jnp.bfloat16).astype(jnp.float32)
        tiled = jnp.concatenate([fields, fields], axis=1)
        applied = (mask_low * tiled).astype(jnp.bfloat16)
        spread = jnp.dot(applied, big_chirp, preferred_element_type=jnp.float32).astype(jnp.bfloat16)
        rotated = jnp.concatenate([-spread[:, cells:], spread[:, :cells]], axis=1)
        arrived = jnp.dot(chirp_real, spread, preferred_element_type=jnp.float32) + jnp.dot(chirp_imag, rotated, preferred_element_type=jnp.float32)
        back_full = back_one.astype(jnp.float32)
        back_real = back_full[:, :cells]
        back_imag = back_full[:, cells:]
        arr_real = arrived[:, :cells]
        arr_imag = arrived[:, cells:]
        term = jnp.concatenate([back_real * arr_real + back_imag * arr_imag, back_imag * arr_real - back_real * arr_imag], axis=1)
        return (running + term, None)
    intersection_two, _ = lax.scan(second_term, jnp.zeros((cells, 2 * cells), jnp.float32), (row_funcs, col_funcs, back_second))
    mask_second = soften(intersection_two * scale_all)
    return (mask_first, mask_second)
```

```python
import functools
import math

import jax
import jax.numpy as jnp
from jax import lax
from jax.experimental import pallas as pl
from jax.experimental.pallas import tpu as pltpu
from jax.sharding import PartitionSpec as P

ORDERS = 32


span_width = 24.0


def grid_points(cells):
    index = jnp.arange(cells, dtype=jnp.float32)
    return (index - cells / 2 + 0.5) * (span_width / cells)


def hermite_table(points):
    before = jnp.zeros_like(points)
    current = math.pi ** (-0.25) * jnp.exp(-0.5 * points * points)
    collected = []
    for order in range(ORDERS):
        collected.append(current)
        following = (
            math.sqrt(2.0 / (order + 1)) * points * current
            - math.sqrt(order / (order + 1.0)) * before
        )
        before, current = (current, following)
    return jnp.stack(collected, axis=0)


def chirp_parts(cells):
    index = jnp.arange(cells, dtype=jnp.int32)
    offset = index[:, None] - index[None, :]
    square = offset * offset % (2 * cells)
    phase = square.astype(jnp.float32) * (math.pi / cells)
    factor = cells ** (-0.5)
    return (
        (jnp.cos(phase) * factor).astype(jnp.bfloat16),
        (jnp.sin(phase) * factor).astype(jnp.bfloat16),
    )


def soften(intersection):
    half = intersection.shape[-1] // 2
    real_part = intersection[..., :half]
    imag_part = intersection[..., half:]
    denom = jnp.sqrt(real_part * real_part + imag_part * imag_part + 1.0)
    return intersection / jnp.concatenate([denom, denom], axis=-1)


def pick_funcs(orders, herm_table):
    one_hot = (orders[:, None] == jnp.arange(herm_table.shape[0], dtype=jnp.int32)[None, :]).astype(
        jnp.float32
    )
    return jnp.dot(one_hot, herm_table, precision=lax.Precision.HIGHEST)


def intersection_first(back_rows, field_rows):
    widened = field_rows.astype(jnp.float32)
    tiled = jnp.concatenate([widened, widened], axis=2)
    return jnp.sum(back_rows.astype(jnp.float32) * tiled, axis=0)


def residue_chirp(cells):
    block = cells // 4
    chirp_real, chirp_imag = chirp_parts(cells)
    index = jnp.arange(block, dtype=jnp.int32)
    residue = (index[None, :] - index[:, None]) % 4
    keep = residue[None] == jnp.arange(4, dtype=jnp.int32)[:, None, None]
    real = jnp.where(keep, chirp_real[None, :block, :block], 0)
    imag = jnp.where(keep, chirp_imag[None, :block, :block], 0)
    return jnp.concatenate(
        [jnp.concatenate([real, imag], axis=2), jnp.concatenate([-imag, real], axis=2)], axis=1
    )


def four_sums(real, imag, sign):
    even_r, even_i = real[0] + real[2], imag[0] + imag[2]
    odd_r, odd_i = real[1] + real[3], imag[1] + imag[3]
    low_r, low_i = real[0] - real[2], imag[0] - imag[2]
    top_r, top_i = sign * (real[1] - real[3]), sign * (imag[1] - imag[3])
    return (
        (even_r + odd_r, even_i + odd_i),
        (low_r - top_i, low_i + top_r),
        (even_r - odd_r, even_i - odd_i),
        (low_r + top_i, low_i - top_r),
    )


def split_four(array, axis):
    return jnp.split(array, 4, axis=axis)


def propagate_columns(real, imag, table):
    block = real.shape[1] // 4
    parts = four_sums(split_four(real, 1), split_four(imag, 1), -1.0)
    outs = []
    for r in range(4):
        both = jnp.concatenate(parts[r], axis=1).astype(jnp.bfloat16)
        outs.append(jnp.dot(both, table[r], preferred_element_type=jnp.float32))
    sums = four_sums([o[:, :block] for o in outs], [o[:, block:] for o in outs], 1.0)
    return [jnp.concatenate([s[k] for s in sums], axis=1).astype(jnp.bfloat16) for k in (0, 1)]


def propagate_down(real, imag, table):
    block = real.shape[0] // 4
    parts = four_sums(
        split_four(real.astype(jnp.float32), 0), split_four(imag.astype(jnp.float32), 0), -1.0
    )
    outs = []
    for r in range(4):
        both = jnp.concatenate(parts[r], axis=0).astype(jnp.bfloat16)
        outs.append(jnp.dot(table[r].T, both, preferred_element_type=jnp.float32))
    sums = four_sums([o[:block] for o in outs], [o[block:] for o in outs], 1.0)
    return [jnp.concatenate([s[k] for s in sums], axis=0) for k in (0, 1)]


MESH = pl.DeviceIdType.MESH
CHUNKS = 4
OFFSETS = (0, 1, 3, 4, 5, 6, 7, 8, 9)
OFFSETS_TWO = (0, 1, 2, 3, 4)


def sweep_kernel(
    depth, scale,
    row_ref, col_ref, chirp_ref, first_hbm, second_hbm, out_one, out_two,
    first, second, sums, from_core, from_near, from_far, from_z,
    sums2, from_core2, from_near2, from_far2, from_z2,
    mask, spread, table_col, table_row, local_sem, send_sem, recv_sem,
):
    cells = first.shape[0]
    chunks, strip, width = sums.shape[0], sums.shape[6], sums.shape[7]
    block = cells // depth
    quarter = cells // 4
    group, sub = lax.axis_index("mgroup"), lax.axis_index("msub")
    z, c = group // 2, group % 2
    y, x = sub // 2, sub % 2
    sibling = (z * 2 + 1 - c, sub)
    across_x = (group, y * 2 + 1 - x)
    across_y = (group, (1 - y) * 2 + x)
    along_z = [(lax.rem(z + i, depth) * 2 + c, sub) for i in range(1, depth)]
    near, far = (x, y), (y, x)
    near_dev, far_dev = (across_x, across_y), (across_y, across_x)

    barrier = pltpu.get_barrier_semaphore()
    for peer in [sibling, across_x, across_y] + along_z:
        pl.semaphore_signal(barrier, inc=1, device_id=peer, device_id_type=MESH)

    loads = {}
    def load(name, src, dst):
        copy = pltpu.make_async_copy(src, dst, local_sem.at[len(loads)])
        copy.start()
        loads[name] = copy
    for k in range(chunks):
        for h in range(2):
            at = pl.ds(h * cells + k * width, width)
            load(("first", k, h), first_hbm.at[:, at], first.at[:, at])
    load("second", second_hbm, second)

    pl.semaphore_wait(barrier, 2 + depth)

    sent = []
    def send(src, dst, peer):
        at = len(sent)
        copy = pltpu.make_async_remote_copy(
            src_ref=src, dst_ref=dst, send_sem=send_sem.at[at], recv_sem=recv_sem.at[at],
            device_id=peer, device_id_type=MESH,
        )
        copy.start()
        sent.append(copy)
        return copy

    def field_at(start, rows, k):
        col = col_ref[:, k * width : (k + 1) * width]
        return (row_ref[pl.ds(start, rows), :] * col).astype(jnp.bfloat16).astype(jnp.float32)

    def soften_pair(real, imag):
        factor = lax.rsqrt(real * real + imag * imag + 1.0)
        return real * factor, imag * factor

    wide = lambda value: value.astype(jnp.float32)
    low = lambda value: value.astype(jnp.bfloat16)
    arrivals = {}

    def reduce_stages(tag, acc, rc, rn, rf, rz):
        def core_send(k):
            for h in range(2):
                arrivals[tag, 0, k, h] = send(acc.at[k, h, 1 - c], rc.at[k, h], sibling)

        def near_send(k):
            for h in range(2):
                arrivals[tag, 0, k, h].wait_recv()
                a = 1 - near[h]
                acc[k, h, c, a] = low(wide(acc[k, h, c, a]) + wide(rc[k, h, a]))
                arrivals[tag, 1, k, h] = send(acc.at[k, h, c, a], rn.at[k, h], near_dev[h])

        def far_send(k):
            for h in range(2):
                arrivals[tag, 1, k, h].wait_recv()
                a, b = near[h], 1 - far[h]
                acc[k, h, c, a, b] = low(
                    wide(acc[k, h, c, a, b]) + wide(rc[k, h, a, b]) + wide(rn[k, h, b])
                )
                arrivals[tag, 2, k, h] = send(acc.at[k, h, c, a, b], rf.at[k, h], far_dev[h])

        def z_send(k):
            for h in range(2):
                arrivals[tag, 2, k, h].wait_recv()
                a, b = near[h], far[h]
                for i in range(1, depth):
                    to = lax.rem(z + i, depth)
                    acc[k, h, c, a, b, to] = low(
                        wide(acc[k, h, c, a, b, to]) + wide(rc[k, h, a, b, to])
                        + wide(rn[k, h, b, to]) + wide(rf[k, h, to])
                    )
                    arrivals[tag, 3, k, h, i] = send(
                        acc.at[k, h, c, a, b, to], rz.at[k, h, i - 1], along_z[i - 1]
                    )

        def finish(k):
            totals = []
            for h in range(2):
                a, b = near[h], far[h]
                total = wide(acc[k, h, c, a, b, z]) + wide(rc[k, h, a, b, z])
                total += wide(rn[k, h, b, z]) + wide(rf[k, h, z])
                for i in range(1, depth):
                    arrivals[tag, 3, k, h, i].wait_recv()
                    total += wide(rz[k, h, i - 1])
                totals.append(total * scale)
            return soften_pair(*totals)

        return core_send, near_send, far_send, z_send, finish

    core_send, near_send, far_send, z_send, finish = reduce_stages(
        1, sums, from_core, from_near, from_far, from_z
    )

    def product(k):
        for h in range(2):
            loads["first", k, h].wait()
        def half(part):
            @pl.loop(0, depth)
            def _(zz):
                for yy in range(2):
                    for xx in range(2):
                        start = pl.multiple_of((((zz * 2 + part) * 2 + yy) * 2 + xx) * strip, strip)
                        field = field_at(start, strip, k)
                        for h in range(2):
                            at = h * cells + k * width
                            value = wide(first[pl.ds(start, strip), at : at + width]) * field
                            a, b = ((xx, yy), (yy, xx))[h]
                            sums[k, h, part, a, b, zz] = low(value)
        half(1 - c)
        core_send(k)
        half(c)

    def first_mask(k):
        real, imag = finish(k)
        for h, value in enumerate((real, imag)):
            at = h * cells + k * width
            out_one[:, at : at + width] = value
            a, b = near[h], far[h]
            mask[k, h, c, a, b, z] = low(value)
            for i in range(1, depth):
                arrivals["g", 0, k, h, i] = send(
                    mask.at[k, h, c, a, b, z], mask.at[k, h, c, a, b, z], along_z[i - 1]
                )

    def gather_far(k):
        for h in range(2):
            for i in range(1, depth):
                arrivals["g", 0, k, h, i].wait_recv()
            at = mask.at[k, h, c, near[h], far[h]]
            arrivals["g", 1, k, h] = send(at, at, far_dev[h])

    def gather_near(k):
        for h in range(2):
            arrivals["g", 1, k, h].wait_recv()
            at = mask.at[k, h, c, near[h]]
            arrivals["g", 2, k, h] = send(at, at, near_dev[h])

    def gather_core(k):
        for h in range(2):
            arrivals["g", 2, k, h].wait_recv()
            at = mask.at[k, h, c]
            arrivals["g", 3, k, h] = send(at, at, sibling)

    def gather_done(k):
        for h in range(2):
            arrivals["g", 3, k, h].wait_recv()

    def schedule(stages, offsets, between=None):
        order = sorted(
            (offsets[s] + k, -s, k) for s in range(len(stages)) for k in range(chunks)
        )
        for n, (_, s, k) in enumerate(order):
            if between and n == 2 * chunks:
                between()
            stages[-s](k)

    def build_tables():
        one = lax.broadcasted_iota(jnp.int32, (quarter, quarter), 0)
        two = lax.broadcasted_iota(jnp.int32, (quarter, quarter), 1)
        real, imag = wide(chirp_ref[0]), wide(chirp_ref[1])
        for table, diff, sign in ((table_col, two - one, 1.0), (table_row, one - two, -1.0)):
            for r in range(4):
                keep = (diff & 3) == r
                rr = jnp.where(keep, real, 0.0)
                ii = jnp.where(keep, imag, 0.0)
                table[r, :quarter, :quarter] = low(rr)
                table[r, quarter:, quarter:] = low(rr)
                table[r, :quarter, quarter:] = low(sign * ii)
                table[r, quarter:, :quarter] = low(-sign * ii)

    schedule(
        (product, near_send, far_send, z_send, first_mask, gather_far, gather_near, gather_core, gather_done),
        OFFSETS, build_tables,
    )

    @pl.loop(0, depth)
    def _(zz):
        start = pl.multiple_of(zz * block, block)
        sides = [[], []]
        for q in range(4):
            field = field_at(start, block, q)
            for h in range(2):
                strips = []
                for cc in range(2):
                    for yy in range(2):
                        for xx in range(2):
                            a, b = ((xx, yy), (yy, xx))[h]
                            strips.append(wide(mask[q, h, cc, a, b, zz]))
                value = jnp.concatenate(strips, axis=0) * field
                sides[h].append(wide(low(value)))
        outs = []
        for r, pair in enumerate(four_sums(sides[0], sides[1], -1.0)):
            both = low(jnp.concatenate(pair, axis=1))
            outs.append(jnp.dot(both, table_col[r], preferred_element_type=jnp.float32))
        done = four_sums([o[:, :quarter] for o in outs], [o[:, quarter:] for o in outs], 1.0)
        for p in range(4):
            for h in range(2):
                spread[p, h, pl.ds(start, block), :] = low(done[p][h])

    core_send2, near_send2, far_send2, z_send2, finish2 = reduce_stages(
        2, sums2, from_core2, from_near2, from_far2, from_z2
    )

    def arrive(k):
        if k == 0:
            loads["second"].wait()
        sides = [
            [wide(spread[k, h, q * quarter : (q + 1) * quarter, :]) for q in range(4)] for h in range(2)
        ]
        outs = []
        for r, pair in enumerate(four_sums(sides[0], sides[1], -1.0)):
            both = low(jnp.concatenate(pair, axis=0))
            outs.append(jnp.dot(table_row[r], both, preferred_element_type=jnp.float32))
        done = four_sums([o[:quarter] for o in outs], [o[quarter:] for o in outs], 1.0)
        for p in range(4):
            rows = slice(p * quarter, (p + 1) * quarter)
            back_real = wide(second[rows, k * width : (k + 1) * width])
            back_imag = wide(second[rows, cells + k * width : cells + (k + 1) * width])
            arr_real, arr_imag = done[p]
            terms = (
                back_real * arr_real + back_imag * arr_imag,
                back_imag * arr_real - back_real * arr_imag,
            )
            for h in range(2):
                value = low(terms[h])
                for n in range(quarter // strip):
                    number = p * (quarter // strip) + n
                    xx, yy, cc, zz = number % 2, number // 2 % 2, number // 4 % 2, number // 8
                    a, b = ((xx, yy), (yy, xx))[h]
                    sums2[k, h, cc, a, b, zz] = value[n * strip : (n + 1) * strip]
        core_send2(k)

    def second_mask(k):
        real, imag = finish2(k)
        out_two[:, k * width : (k + 1) * width] = real
        out_two[:, cells + k * width : cells + (k + 1) * width] = imag

    schedule((arrive, near_send2, far_send2, z_send2, second_mask), OFFSETS_TWO)
    for copy in sent:
        copy.wait_send()


def sweep_call(row_func, col_func, chirp, back_first, back_second, devices, depth, scale):
    cells = back_first.shape[0]
    strip, width, chunks = cells // devices, cells // CHUNKS, CHUNKS
    low = jnp.bfloat16
    tail = (strip, width)
    received = [
        pltpu.VMEM((chunks, 2, 2, 2, depth) + tail, low),
        pltpu.VMEM((chunks, 2, 2, depth) + tail, low),
        pltpu.VMEM((chunks, 2, depth) + tail, low),
        pltpu.VMEM((chunks, 2, depth - 1) + tail, low),
    ]
    whole = pltpu.VMEM((chunks, 2, 2, 2, 2, depth) + tail, low)
    table = pltpu.VMEM((4, cells // 2, cells // 2), low)
    copies = 3 * chunks * 2 * (3 + depth - 1)
    vmem = pl.BlockSpec(memory_space=pltpu.VMEM)
    hbm = pl.BlockSpec(memory_space=pl.ANY)
    out = jax.ShapeDtypeStruct((strip, 2 * cells), jnp.float32)
    return pl.pallas_call(
        functools.partial(sweep_kernel, depth, scale),
        out_shape=(out, out),
        in_specs=[vmem, vmem, vmem, hbm, hbm],
        out_specs=(vmem, vmem),
        scratch_shapes=[pltpu.VMEM((cells, 2 * cells), low)] * 2
        + [whole] + received + [whole] + received
        + [whole, pltpu.VMEM((CHUNKS, 2, cells, width), low), table, table]
        + [
            pltpu.SemaphoreType.DMA((2 * chunks + 1,)),
            pltpu.SemaphoreType.DMA((copies,)),
            pltpu.SemaphoreType.DMA((copies,)),
        ],
        compiler_params=pltpu.CompilerParams(
            collective_id=0, has_side_effects=True, vmem_limit_bytes=60 * 1024 * 1024
        ),
        name="sweep",
    )(row_func, col_func, chirp, back_first, back_second)


def body(in_modes, back_first, back_second):
    mode_dev = in_modes.shape[0]
    cells = back_first.shape[1]
    axes = ("mgroup", "msub")
    devices_all = lax.axis_size("mgroup") * lax.axis_size("msub")
    scale_all = float(mode_dev * devices_all) ** (-0.5)
    herm_table = hermite_table(grid_points(cells))
    row_funcs = pick_funcs(in_modes[:, 0], herm_table)
    col_funcs = pick_funcs(in_modes[:, 1], herm_table)
    depth = lax.axis_size("mgroup") // 2
    if mode_dev == 1 and lax.axis_size("msub") == 4 and depth == 4 and cells % (16 * devices_all) == 0:
        block = cells // 4
        chirp = jnp.stack([part[:block, :block] for part in chirp_parts(cells)])
        return sweep_call(
            row_funcs.T, col_funcs, chirp, back_first[0], back_second[0], devices_all, depth, scale_all
        )
    fields = (row_funcs[:, :, None] * col_funcs[:, None, :]).astype(jnp.bfloat16)
    table = residue_chirp(cells)
    first = intersection_first(back_first, fields).astype(jnp.bfloat16)
    summed = lax.psum_scatter(first, axes, scatter_dimension=0, tiled=True)
    mask_first = soften(summed.astype(jnp.float32) * scale_all)
    full_mask = lax.all_gather(mask_first.astype(jnp.bfloat16), axes, axis=0, tiled=True)
    full_mask = full_mask.astype(jnp.float32)
    real_part, imag_part = 0.0, 0.0
    for mode in range(mode_dev):
        field = fields[mode].astype(jnp.float32)
        real = (full_mask[:, :cells] * field).astype(jnp.bfloat16).astype(jnp.float32)
        imag = (full_mask[:, cells:] * field).astype(jnp.bfloat16).astype(jnp.float32)
        arr_real, arr_imag = propagate_down(*propagate_columns(real, imag, table), table)
        back = back_second[mode].astype(jnp.float32)
        back_real, back_imag = back[:, :cells], back[:, cells:]
        real_part += back_real * arr_real + back_imag * arr_imag
        imag_part += back_imag * arr_real - back_real * arr_imag
    second = jnp.concatenate([real_part, imag_part], axis=1).astype(jnp.bfloat16)
    summed_two = lax.psum_scatter(second, axes, scatter_dimension=0, tiled=True)
    mask_second = soften(summed_two.astype(jnp.float32) * scale_all)
    return (mask_first, mask_second)


def solution(mesh):
    placed = (
        P(("mgroup", "msub"), None),
        P(("mgroup", "msub"), None, None),
        P(("mgroup", "msub"), None, None),
    )
    return jax.shard_map(
        body,
        mesh=mesh,
        in_specs=placed,
        out_specs=(P(("mgroup", "msub"), None), P(("mgroup", "msub"), None)),
        check_vma=False,
    )
```

```python
import functools
import math

import jax
import jax.numpy as jnp
from jax import lax
from jax.experimental import pallas as pl
from jax.experimental.pallas import tpu as pltpu
from jax.sharding import PartitionSpec as P

ORDERS = 32


span_width = 24.0


def grid_points(cells):
    index = jnp.arange(cells, dtype=jnp.float32)
    return (index - cells / 2 + 0.5) * (span_width / cells)


def hermite_table(points):
    before = jnp.zeros_like(points)
    current = math.pi ** (-0.25) * jnp.exp(-0.5 * points * points)
    collected = []
    for order in range(ORDERS):
        collected.append(current)
        following = (
            math.sqrt(2.0 / (order + 1)) * points * current
            - math.sqrt(order / (order + 1.0)) * before
        )
        before, current = (current, following)
    return jnp.stack(collected, axis=0)


def chirp_parts(cells):
    index = jnp.arange(cells, dtype=jnp.int32)
    offset = index[:, None] - index[None, :]
    square = offset * offset % (2 * cells)
    phase = square.astype(jnp.float32) * (math.pi / cells)
    factor = cells ** (-0.5)
    return (
        (jnp.cos(phase) * factor).astype(jnp.bfloat16),
        (jnp.sin(phase) * factor).astype(jnp.bfloat16),
    )


def soften(intersection):
    half = intersection.shape[-1] // 2
    real_part = intersection[..., :half]
    imag_part = intersection[..., half:]
    denom = jnp.sqrt(real_part * real_part + imag_part * imag_part + 1.0)
    return intersection / jnp.concatenate([denom, denom], axis=-1)


def pick_funcs(orders, herm_table):
    one_hot = (orders[:, None] == jnp.arange(herm_table.shape[0], dtype=jnp.int32)[None, :]).astype(
        jnp.float32
    )
    return jnp.dot(one_hot, herm_table, precision=lax.Precision.HIGHEST)


def intersection_first(back_rows, field_rows):
    widened = field_rows.astype(jnp.float32)
    tiled = jnp.concatenate([widened, widened], axis=2)
    return jnp.sum(back_rows.astype(jnp.float32) * tiled, axis=0)


def residue_chirp(cells):
    block = cells // 4
    chirp_real, chirp_imag = chirp_parts(cells)
    index = jnp.arange(block, dtype=jnp.int32)
    residue = (index[None, :] - index[:, None]) % 4
    keep = residue[None] == jnp.arange(4, dtype=jnp.int32)[:, None, None]
    real = jnp.where(keep, chirp_real[None, :block, :block], 0)
    imag = jnp.where(keep, chirp_imag[None, :block, :block], 0)
    return jnp.concatenate(
        [jnp.concatenate([real, imag], axis=2), jnp.concatenate([-imag, real], axis=2)], axis=1
    )


def four_sums(real, imag, sign):
    even_r, even_i = real[0] + real[2], imag[0] + imag[2]
    odd_r, odd_i = real[1] + real[3], imag[1] + imag[3]
    low_r, low_i = real[0] - real[2], imag[0] - imag[2]
    top_r, top_i = sign * (real[1] - real[3]), sign * (imag[1] - imag[3])
    return (
        (even_r + odd_r, even_i + odd_i),
        (low_r - top_i, low_i + top_r),
        (even_r - odd_r, even_i - odd_i),
        (low_r + top_i, low_i - top_r),
    )


def split_four(array, axis):
    return jnp.split(array, 4, axis=axis)


def propagate_columns(real, imag, table):
    block = real.shape[1] // 4
    parts = four_sums(split_four(real, 1), split_four(imag, 1), -1.0)
    outs = []
    for r in range(4):
        both = jnp.concatenate(parts[r], axis=1).astype(jnp.bfloat16)
        outs.append(jnp.dot(both, table[r], preferred_element_type=jnp.float32))
    sums = four_sums([o[:, :block] for o in outs], [o[:, block:] for o in outs], 1.0)
    return [jnp.concatenate([s[k] for s in sums], axis=1).astype(jnp.bfloat16) for k in (0, 1)]


def propagate_down(real, imag, table):
    block = real.shape[0] // 4
    parts = four_sums(
        split_four(real.astype(jnp.float32), 0), split_four(imag.astype(jnp.float32), 0), -1.0
    )
    outs = []
    for r in range(4):
        both = jnp.concatenate(parts[r], axis=0).astype(jnp.bfloat16)
        outs.append(jnp.dot(table[r].T, both, preferred_element_type=jnp.float32))
    sums = four_sums([o[:block] for o in outs], [o[block:] for o in outs], 1.0)
    return [jnp.concatenate([s[k] for s in sums], axis=0) for k in (0, 1)]


MESH = pl.DeviceIdType.MESH
CHUNKS = 4
OFFSETS = (0, 1, 3, 4, 5, 6, 7, 9, 10)
OFFSETS_TWO = (0, 1, 2, 3, 4)


def sweep_kernel(
    depth, scale,
    modes_ref, first_hbm, second_hbm, out_one, out_two,
    first, second, sums, from_core, from_near, from_far, from_z,
    sums2, from_core2, from_near2, from_far2, from_z2,
    mask, applied, spread, table_col, table_row, row_ref, col_ref, local_sem, send_sem, recv_sem,
):
    cells = first.shape[0]
    chunks, strip, width = sums.shape[0], sums.shape[6], sums.shape[7]
    block = cells // depth
    quarter = cells // 4
    group, sub = lax.axis_index("mgroup"), lax.axis_index("msub")
    z, c = group // 2, group % 2
    y, x = sub // 2, sub % 2
    sibling = (z * 2 + 1 - c, sub)
    across_x = (group, y * 2 + 1 - x)
    across_y = (group, (1 - y) * 2 + x)
    along_z = [(lax.rem(z + i, depth) * 2 + c, sub) for i in range(1, depth)]
    near, far = (x, y), (y, x)
    near_dev, far_dev = (across_x, across_y), (across_y, across_x)

    barrier = pltpu.get_barrier_semaphore()
    for peer in [sibling, across_x, across_y] + along_z:
        pl.semaphore_signal(barrier, inc=1, device_id=peer, device_id_type=MESH)

    loads = {}
    def load(name, src, dst):
        copy = pltpu.make_async_copy(src, dst, local_sem.at[len(loads)])
        copy.start()
        loads[name] = copy
    for k in range(chunks):
        for h in range(2):
            at = pl.ds(h * cells + k * width, width)
            load(("first", k, h), first_hbm.at[:, at], first.at[:, at])
    load("second", second_hbm, second)

    lanes = row_ref.shape[1]
    index = lax.broadcasted_iota(jnp.int32, (8, cells), 1).astype(jnp.float32)
    points = (index - cells / 2 + 0.5) * (span_width / cells)
    orders = modes_ref[...]
    row_order, col_order = orders[0:1], orders[1:2]
    before, current = jnp.zeros_like(points), math.pi ** (-0.25) * jnp.exp(-0.5 * points * points)
    row_func, col_func = before, before
    for order in range(ORDERS):
        row_func = jnp.where(row_order == order, current, row_func)
        col_func = jnp.where(col_order == order, current, col_func)
        before, current = current, (
            math.sqrt(2.0 / (order + 1)) * points * current
            - math.sqrt(order / (order + 1.0)) * before
        )
    col_ref[...] = col_func[:1]
    row_ref[...] = jnp.broadcast_to(row_func[:1], (lanes, cells)).T

    pl.semaphore_wait(barrier, 2 + depth)

    sent = []
    def send(src, dst, peer):
        at = len(sent)
        copy = pltpu.make_async_remote_copy(
            src_ref=src, dst_ref=dst, send_sem=send_sem.at[at], recv_sem=recv_sem.at[at],
            device_id=peer, device_id_type=MESH,
        )
        copy.start()
        sent.append(copy)
        return copy

    def field_at(start, rows, k):
        col = col_ref[:, k * width : (k + 1) * width]
        row = jnp.concatenate([row_ref[pl.ds(start, rows), :]] * (width // lanes), axis=1)
        return (row * col).astype(jnp.bfloat16).astype(jnp.float32)

    def soften_pair(real, imag):
        factor = lax.rsqrt(real * real + imag * imag + 1.0)
        return real * factor, imag * factor

    wide = lambda value: value.astype(jnp.float32)
    low = lambda value: value.astype(jnp.bfloat16)
    arrivals = {}

    def reduce_stages(tag, acc, rc, rn, rf, rz):
        def core_send(k):
            for h in range(2):
                arrivals[tag, 0, k, h] = send(acc.at[k, h, 1 - c], rc.at[k, h], sibling)

        def near_send(k):
            for h in range(2):
                arrivals[tag, 0, k, h].wait_recv()
                a = 1 - near[h]
                acc[k, h, c, a] = low(wide(acc[k, h, c, a]) + wide(rc[k, h, a]))
                arrivals[tag, 1, k, h] = send(acc.at[k, h, c, a], rn.at[k, h], near_dev[h])

        def far_send(k):
            for h in range(2):
                arrivals[tag, 1, k, h].wait_recv()
                a, b = near[h], 1 - far[h]
                acc[k, h, c, a, b] = low(
                    wide(acc[k, h, c, a, b]) + wide(rc[k, h, a, b]) + wide(rn[k, h, b])
                )
                arrivals[tag, 2, k, h] = send(acc.at[k, h, c, a, b], rf.at[k, h], far_dev[h])

        def z_send(k):
            for h in range(2):
                arrivals[tag, 2, k, h].wait_recv()
                a, b = near[h], far[h]
                for i in range(1, depth):
                    to = lax.rem(z + i, depth)
                    acc[k, h, c, a, b, to] = low(
                        wide(acc[k, h, c, a, b, to]) + wide(rc[k, h, a, b, to])
                        + wide(rn[k, h, b, to]) + wide(rf[k, h, to])
                    )
                    arrivals[tag, 3, k, h, i] = send(
                        acc.at[k, h, c, a, b, to], rz.at[k, h, i - 1], along_z[i - 1]
                    )

        def finish(k):
            totals = []
            for h in range(2):
                a, b = near[h], far[h]
                total = wide(acc[k, h, c, a, b, z]) + wide(rc[k, h, a, b, z])
                total += wide(rn[k, h, b, z]) + wide(rf[k, h, z])
                for i in range(1, depth):
                    arrivals[tag, 3, k, h, i].wait_recv()
                    total += wide(rz[k, h, i - 1])
                totals.append(total * scale)
            return soften_pair(*totals)

        return core_send, near_send, far_send, z_send, finish

    core_send, near_send, far_send, z_send, finish = reduce_stages(
        1, sums, from_core, from_near, from_far, from_z
    )

    def product(k):
        for h in range(2):
            loads["first", k, h].wait()
        def half(part):
            @pl.loop(0, depth)
            def _(zz):
                for yy in range(2):
                    for xx in range(2):
                        start = pl.multiple_of((((zz * 2 + part) * 2 + yy) * 2 + xx) * strip, strip)
                        field = field_at(start, strip, k)
                        for h in range(2):
                            at = h * cells + k * width
                            value = wide(first[pl.ds(start, strip), at : at + width]) * field
                            a, b = ((xx, yy), (yy, xx))[h]
                            sums[k, h, part, a, b, zz] = low(value)
        half(1 - c)
        core_send(k)
        half(c)

    def first_mask(k):
        real, imag = finish(k)
        for h, value in enumerate((real, imag)):
            at = h * cells + k * width
            out_one[:, at : at + width] = value
            a, b = near[h], far[h]
            mask[k, h, c, a, b, z] = low(value)
            for i in range(1, depth):
                arrivals["g", 0, k, h, i] = send(
                    mask.at[k, h, c, a, b, z], mask.at[k, h, c, a, b, z], along_z[i - 1]
                )

    def gather_far(k):
        for h in range(2):
            for i in range(1, depth):
                arrivals["g", 0, k, h, i].wait_recv()
            at = mask.at[k, h, c, near[h], far[h]]
            arrivals["g", 1, k, h] = send(at, at, far_dev[h])

    def gather_near(k):
        for h in range(2):
            arrivals["g", 1, k, h].wait_recv()
            at = mask.at[k, h, c, near[h]]
            arrivals["g", 2, k, h] = send(at, at, near_dev[h])

    def gather_core(k):
        for h in range(2):
            arrivals["g", 2, k, h].wait_recv()
            at = mask.at[k, h, c]
            arrivals["g", 3, k, h] = send(at, at, sibling)

    def gather_done(k):
        for h in range(2):
            arrivals["g", 3, k, h].wait_recv()

        @pl.loop(0, depth)
        def _(zz):
            for cc in range(2):
                for yy in range(2):
                    for xx in range(2):
                        start = pl.multiple_of((((zz * 2 + cc) * 2 + yy) * 2 + xx) * strip, strip)
                        field = field_at(start, strip, k)
                        for h in range(2):
                            a, b = ((xx, yy), (yy, xx))[h]
                            applied[k, h, pl.ds(start, strip), :] = low(
                                wide(mask[k, h, cc, a, b, zz]) * field
                            )

    def schedule(stages, offsets, between=None):
        order = sorted(
            (offsets[s] + k, -s, k) for s in range(len(stages)) for k in range(chunks)
        )
        for n, (_, s, k) in enumerate(order):
            if between and n == 2 * chunks:
                between()
            stages[-s](k)

    def build_tables():
        one = lax.broadcasted_iota(jnp.int32, (quarter, quarter), 0)
        two = lax.broadcasted_iota(jnp.int32, (quarter, quarter), 1)
        square = lax.rem((one - two) * (one - two), 2 * cells)
        phase = square.astype(jnp.float32) * (math.pi / cells)
        factor = cells ** (-0.5)
        real, imag = wide(low(jnp.cos(phase) * factor)), wide(low(jnp.sin(phase) * factor))
        for table, diff, sign in ((table_col, two - one, 1.0), (table_row, one - two, -1.0)):
            for r in range(4):
                keep = (diff & 3) == r
                rr = jnp.where(keep, real, 0.0)
                ii = jnp.where(keep, imag, 0.0)
                table[r, :quarter, :quarter] = low(rr)
                table[r, quarter:, quarter:] = low(rr)
                table[r, :quarter, quarter:] = low(sign * ii)
                table[r, quarter:, :quarter] = low(-sign * ii)

    schedule(
        (product, near_send, far_send, z_send, first_mask, gather_far, gather_near, gather_core, gather_done),
        OFFSETS, build_tables,
    )

    @pl.loop(0, depth)
    def _(zz):
        start = pl.multiple_of(zz * block, block)
        sides = [
            [wide(applied[q, h, pl.ds(start, block), :]) for q in range(4)] for h in range(2)
        ]
        outs = []
        for r, pair in enumerate(four_sums(sides[0], sides[1], -1.0)):
            both = low(jnp.concatenate(pair, axis=1))
            outs.append(jnp.dot(both, table_col[r], preferred_element_type=jnp.float32))
        done = four_sums([o[:, :quarter] for o in outs], [o[:, quarter:] for o in outs], 1.0)
        for p in range(4):
            for h in range(2):
                spread[p, h, pl.ds(start, block), :] = low(done[p][h])

    core_send2, near_send2, far_send2, z_send2, finish2 = reduce_stages(
        2, sums2, from_core2, from_near2, from_far2, from_z2
    )

    def arrive(k):
        if k == 0:
            loads["second"].wait()
        sides = [
            [wide(spread[k, h, q * quarter : (q + 1) * quarter, :]) for q in range(4)] for h in range(2)
        ]
        outs = []
        for r, pair in enumerate(four_sums(sides[0], sides[1], -1.0)):
            both = low(jnp.concatenate(pair, axis=0))
            outs.append(jnp.dot(table_row[r], both, preferred_element_type=jnp.float32))
        done = four_sums([o[:quarter] for o in outs], [o[quarter:] for o in outs], 1.0)
        for p in range(4):
            rows = slice(p * quarter, (p + 1) * quarter)
            back_real = wide(second[rows, k * width : (k + 1) * width])
            back_imag = wide(second[rows, cells + k * width : cells + (k + 1) * width])
            arr_real, arr_imag = done[p]
            terms = (
                back_real * arr_real + back_imag * arr_imag,
                back_imag * arr_real - back_real * arr_imag,
            )
            for h in range(2):
                value = low(terms[h])
                for n in range(quarter // strip):
                    number = p * (quarter // strip) + n
                    xx, yy, cc, zz = number % 2, number // 2 % 2, number // 4 % 2, number // 8
                    a, b = ((xx, yy), (yy, xx))[h]
                    sums2[k, h, cc, a, b, zz] = value[n * strip : (n + 1) * strip]
        core_send2(k)

    def second_mask(k):
        real, imag = finish2(k)
        out_two[:, k * width : (k + 1) * width] = real
        out_two[:, cells + k * width : cells + (k + 1) * width] = imag

    schedule((arrive, near_send2, far_send2, z_send2, second_mask), OFFSETS_TWO)
    for copy in sent:
        copy.wait_send()


def hand_on_kernel(one_in, two_in, one_out, two_out, sem):
    copies = [
        pltpu.make_async_copy(one_in, one_out, sem.at[0]),
        pltpu.make_async_copy(two_in, two_out, sem.at[1]),
    ]
    for copy in copies:
        copy.start()
    for copy in copies:
        copy.wait()


def sweep_call(modes, back_first, back_second, devices, depth, scale):
    cells = back_first.shape[0]
    strip, width, chunks = cells // devices, cells // CHUNKS, CHUNKS
    low = jnp.bfloat16
    tail = (strip, width)
    received = [
        pltpu.VMEM((chunks, 2, 2, 2, depth) + tail, low),
        pltpu.VMEM((chunks, 2, 2, depth) + tail, low),
        pltpu.VMEM((chunks, 2, depth) + tail, low),
        pltpu.VMEM((chunks, 2, depth - 1) + tail, low),
    ]
    whole = pltpu.VMEM((chunks, 2, 2, 2, 2, depth) + tail, low)
    table = pltpu.VMEM((4, cells // 2, cells // 2), low)
    copies = 3 * chunks * 2 * (3 + depth - 1)
    vmem = pl.BlockSpec(memory_space=pltpu.VMEM)
    hbm = pl.BlockSpec(memory_space=pl.ANY)
    out = jax.ShapeDtypeStruct((strip, 2 * cells), jnp.float32)
    swept = pl.pallas_call(
        functools.partial(sweep_kernel, depth, scale),
        out_shape=(out, out),
        in_specs=[vmem, hbm, hbm],
        out_specs=(vmem, vmem),
        scratch_shapes=[pltpu.VMEM((cells, 2 * cells), low)] * 2
        + [whole] + received + [whole] + received
        + [whole] + [pltpu.VMEM((CHUNKS, 2, cells, width), low)] * 2 + [table, table]
        + [pltpu.VMEM((cells, 128), jnp.float32), pltpu.VMEM((1, cells), jnp.float32)]
        + [
            pltpu.SemaphoreType.DMA((2 * chunks + 1,)),
            pltpu.SemaphoreType.DMA((copies,)),
            pltpu.SemaphoreType.DMA((copies,)),
        ],
        compiler_params=pltpu.CompilerParams(
            collective_id=0, has_side_effects=True, vmem_limit_bytes=60 * 1024 * 1024
        ),
        name="sweep",
    )(modes, back_first, back_second)
    return pl.pallas_call(
        hand_on_kernel,
        out_shape=(out, out),
        in_specs=[hbm, hbm],
        out_specs=(hbm, hbm),
        scratch_shapes=[pltpu.SemaphoreType.DMA((2,))],
        compiler_params=pltpu.CompilerParams(vmem_limit_bytes=63 * 1024 * 1024),
        name="hand_on",
    )(*swept)


def body(in_modes, back_first, back_second):
    mode_dev = in_modes.shape[0]
    cells = back_first.shape[1]
    axes = ("mgroup", "msub")
    devices_all = lax.axis_size("mgroup") * lax.axis_size("msub")
    scale_all = float(mode_dev * devices_all) ** (-0.5)
    depth = lax.axis_size("mgroup") // 2
    if mode_dev == 1 and lax.axis_size("msub") == 4 and depth == 4 and cells % (16 * devices_all) == 0:
        return sweep_call(
            in_modes.T, back_first[0], back_second[0], devices_all, depth, scale_all
        )
    herm_table = hermite_table(grid_points(cells))
    row_funcs = pick_funcs(in_modes[:, 0], herm_table)
    col_funcs = pick_funcs(in_modes[:, 1], herm_table)
    fields = (row_funcs[:, :, None] * col_funcs[:, None, :]).astype(jnp.bfloat16)
    table = residue_chirp(cells)
    first = intersection_first(back_first, fields).astype(jnp.bfloat16)
    summed = lax.psum_scatter(first, axes, scatter_dimension=0, tiled=True)
    mask_first = soften(summed.astype(jnp.float32) * scale_all)
    full_mask = lax.all_gather(mask_first.astype(jnp.bfloat16), axes, axis=0, tiled=True)
    full_mask = full_mask.astype(jnp.float32)
    real_part, imag_part = 0.0, 0.0
    for mode in range(mode_dev):
        field = fields[mode].astype(jnp.float32)
        real = (full_mask[:, :cells] * field).astype(jnp.bfloat16).astype(jnp.float32)
        imag = (full_mask[:, cells:] * field).astype(jnp.bfloat16).astype(jnp.float32)
        arr_real, arr_imag = propagate_down(*propagate_columns(real, imag, table), table)
        back = back_second[mode].astype(jnp.float32)
        back_real, back_imag = back[:, :cells], back[:, cells:]
        real_part += back_real * arr_real + back_imag * arr_imag
        imag_part += back_imag * arr_real - back_real * arr_imag
    second = jnp.concatenate([real_part, imag_part], axis=1).astype(jnp.bfloat16)
    summed_two = lax.psum_scatter(second, axes, scatter_dimension=0, tiled=True)
    mask_second = soften(summed_two.astype(jnp.float32) * scale_all)
    return (mask_first, mask_second)


def solution(mesh):
    placed = (
        P(("mgroup", "msub"), None),
        P(("mgroup", "msub"), None, None),
        P(("mgroup", "msub"), None, None),
    )
    return jax.shard_map(
        body,
        mesh=mesh,
        in_specs=placed,
        out_specs=(P(("mgroup", "msub"), None), P(("mgroup", "msub"), None)),
        check_vma=False,
    )
```

```python
import functools
import math

import jax
import jax.numpy as jnp
from jax import lax
from jax.experimental import pallas as pl
from jax.experimental.pallas import tpu as pltpu
from jax.sharding import PartitionSpec as P

ORDERS = 32


span_width = 24.0


def grid_points(cells):
    index = jnp.arange(cells, dtype=jnp.float32)
    return (index - cells / 2 + 0.5) * (span_width / cells)


def hermite_table(points):
    before = jnp.zeros_like(points)
    current = math.pi ** (-0.25) * jnp.exp(-0.5 * points * points)
    collected = []
    for order in range(ORDERS):
        collected.append(current)
        following = (
            math.sqrt(2.0 / (order + 1)) * points * current
            - math.sqrt(order / (order + 1.0)) * before
        )
        before, current = (current, following)
    return jnp.stack(collected, axis=0)


def chirp_parts(cells):
    index = jnp.arange(cells, dtype=jnp.int32)
    offset = index[:, None] - index[None, :]
    square = offset * offset % (2 * cells)
    phase = square.astype(jnp.float32) * (math.pi / cells)
    factor = cells ** (-0.5)
    return (
        (jnp.cos(phase) * factor).astype(jnp.bfloat16),
        (jnp.sin(phase) * factor).astype(jnp.bfloat16),
    )


def soften(intersection):
    half = intersection.shape[-1] // 2
    real_part = intersection[..., :half]
    imag_part = intersection[..., half:]
    denom = jnp.sqrt(real_part * real_part + imag_part * imag_part + 1.0)
    return intersection / jnp.concatenate([denom, denom], axis=-1)


def pick_funcs(orders, herm_table):
    one_hot = (orders[:, None] == jnp.arange(herm_table.shape[0], dtype=jnp.int32)[None, :]).astype(
        jnp.float32
    )
    return jnp.dot(one_hot, herm_table, precision=lax.Precision.HIGHEST)


def intersection_first(back_rows, field_rows):
    widened = field_rows.astype(jnp.float32)
    tiled = jnp.concatenate([widened, widened], axis=2)
    return jnp.sum(back_rows.astype(jnp.float32) * tiled, axis=0)


def residue_chirp(cells):
    block = cells // 4
    chirp_real, chirp_imag = chirp_parts(cells)
    index = jnp.arange(block, dtype=jnp.int32)
    residue = (index[None, :] - index[:, None]) % 4
    keep = residue[None] == jnp.arange(4, dtype=jnp.int32)[:, None, None]
    real = jnp.where(keep, chirp_real[None, :block, :block], 0)
    imag = jnp.where(keep, chirp_imag[None, :block, :block], 0)
    return jnp.concatenate(
        [jnp.concatenate([real, imag], axis=2), jnp.concatenate([-imag, real], axis=2)], axis=1
    )


def four_sums(real, imag, sign):
    even_r, even_i = real[0] + real[2], imag[0] + imag[2]
    odd_r, odd_i = real[1] + real[3], imag[1] + imag[3]
    low_r, low_i = real[0] - real[2], imag[0] - imag[2]
    top_r, top_i = sign * (real[1] - real[3]), sign * (imag[1] - imag[3])
    return (
        (even_r + odd_r, even_i + odd_i),
        (low_r - top_i, low_i + top_r),
        (even_r - odd_r, even_i - odd_i),
        (low_r + top_i, low_i - top_r),
    )


def split_four(array, axis):
    return jnp.split(array, 4, axis=axis)


def propagate_columns(real, imag, table):
    block = real.shape[1] // 4
    parts = four_sums(split_four(real, 1), split_four(imag, 1), -1.0)
    outs = []
    for r in range(4):
        both = jnp.concatenate(parts[r], axis=1).astype(jnp.bfloat16)
        outs.append(jnp.dot(both, table[r], preferred_element_type=jnp.float32))
    sums = four_sums([o[:, :block] for o in outs], [o[:, block:] for o in outs], 1.0)
    return [jnp.concatenate([s[k] for s in sums], axis=1).astype(jnp.bfloat16) for k in (0, 1)]


def propagate_down(real, imag, table):
    block = real.shape[0] // 4
    parts = four_sums(
        split_four(real.astype(jnp.float32), 0), split_four(imag.astype(jnp.float32), 0), -1.0
    )
    outs = []
    for r in range(4):
        both = jnp.concatenate(parts[r], axis=0).astype(jnp.bfloat16)
        outs.append(jnp.dot(table[r].T, both, preferred_element_type=jnp.float32))
    sums = four_sums([o[:block] for o in outs], [o[block:] for o in outs], 1.0)
    return [jnp.concatenate([s[k] for s in sums], axis=0) for k in (0, 1)]


MESH = pl.DeviceIdType.MESH
CHUNKS = 8
KEYS = (
    (0.3, 0.7), (1.1, 0.9), (2.8, 0.9), (3.7, 1.0), (5.2, 1.0),
    (7.0, 0.9), (8.9, 0.8), (11.5, 0.8), (12.7, 1.1),
)
KEYS_TWO = ((0.0, 0.5), (1.4, 0.5), (3.3, 0.3), (3.9, 0.3), (22.7, 6.4))


def sweep_kernel(
    depth, scale,
    modes_ref, first_hbm, second_hbm, out_one, out_two,
    first, second, sums, from_core, from_near, from_far, from_z,
    sums2, from_core2, from_near2, from_far2, from_z2,
    mask, applied, spread, table_col, table_row, row_ref, col_ref, local_sem, send_sem, recv_sem,
):
    cells = first.shape[0]
    chunks, strip, width = sums.shape[0], sums.shape[6], sums.shape[7]
    block = cells // depth
    quarter = cells // 4
    pieces = quarter // width
    group, sub = lax.axis_index("mgroup"), lax.axis_index("msub")
    z, c = group // 2, group % 2
    y, x = sub // 2, sub % 2
    sibling = (z * 2 + 1 - c, sub)
    across_x = (group, y * 2 + 1 - x)
    across_y = (group, (1 - y) * 2 + x)
    along_z = [(lax.rem(z + i, depth) * 2 + c, sub) for i in range(1, depth)]
    near, far = (x, y), (y, x)
    near_dev, far_dev = (across_x, across_y), (across_y, across_x)

    barrier = pltpu.get_barrier_semaphore()
    for peer in [sibling, across_x, across_y] + along_z:
        pl.semaphore_signal(barrier, inc=1, device_id=peer, device_id_type=MESH)

    loads = {}
    def load(name, src, dst):
        copy = pltpu.make_async_copy(src, dst, local_sem.at[len(loads)])
        copy.start()
        loads[name] = copy
    for k in range(chunks):
        for h in range(2):
            at = pl.ds(h * cells + k * width, width)
            load(("first", k, h), first_hbm.at[:, at], first.at[:, at])
    load("second", second_hbm, second)

    lanes = row_ref.shape[1]
    index = lax.broadcasted_iota(jnp.int32, (8, cells), 1).astype(jnp.float32)
    points = (index - cells / 2 + 0.5) * (span_width / cells)
    orders = modes_ref[...]
    row_order, col_order = orders[:, 0:1], orders[:, 1:2]
    before, current = jnp.zeros_like(points), math.pi ** (-0.25) * jnp.exp(-0.5 * points * points)
    row_func, col_func = before, before
    for order in range(ORDERS):
        row_func = jnp.where(row_order == order, current, row_func)
        col_func = jnp.where(col_order == order, current, col_func)
        before, current = current, (
            math.sqrt(2.0 / (order + 1)) * points * current
            - math.sqrt(order / (order + 1.0)) * before
        )
    col_ref[...] = col_func[:1]
    row_ref[...] = jnp.broadcast_to(row_func[:1], (lanes, cells)).T

    pl.semaphore_wait(barrier, 2 + depth)

    sent = []
    def send(src, dst, peer):
        at = len(sent)
        copy = pltpu.make_async_remote_copy(
            src_ref=src, dst_ref=dst, send_sem=send_sem.at[at], recv_sem=recv_sem.at[at],
            device_id=peer, device_id_type=MESH,
        )
        copy.start()
        sent.append(copy)
        return copy

    def field_at(start, rows, k):
        col = col_ref[:, k * width : (k + 1) * width]
        row = jnp.concatenate([row_ref[pl.ds(start, rows), :]] * (width // lanes), axis=1)
        return (row * col).astype(jnp.bfloat16).astype(jnp.float32)

    def soften_pair(real, imag):
        factor = lax.rsqrt(real * real + imag * imag + 1.0)
        return real * factor, imag * factor

    wide = lambda value: value.astype(jnp.float32)
    low = lambda value: value.astype(jnp.bfloat16)
    arrivals = {}

    def reduce_stages(tag, acc, rc, rn, rf, rz):
        def core_send(k):
            for h in range(2):
                arrivals[tag, 0, k, h] = send(acc.at[k, h, 1 - c], rc.at[k, h], sibling)

        def near_send(k):
            for h in range(2):
                arrivals[tag, 0, k, h].wait_recv()
                a = 1 - near[h]
                acc[k, h, c, a] = low(wide(acc[k, h, c, a]) + wide(rc[k, h, a]))
                arrivals[tag, 1, k, h] = send(acc.at[k, h, c, a], rn.at[k, h], near_dev[h])

        def far_send(k):
            for h in range(2):
                arrivals[tag, 1, k, h].wait_recv()
                a, b = near[h], 1 - far[h]
                acc[k, h, c, a, b] = low(
                    wide(acc[k, h, c, a, b]) + wide(rc[k, h, a, b]) + wide(rn[k, h, b])
                )
                arrivals[tag, 2, k, h] = send(acc.at[k, h, c, a, b], rf.at[k, h], far_dev[h])

        def z_send(k):
            for h in range(2):
                arrivals[tag, 2, k, h].wait_recv()
                a, b = near[h], far[h]
                for i in range(1, depth):
                    to = lax.rem(z + i, depth)
                    acc[k, h, c, a, b, to] = low(
                        wide(acc[k, h, c, a, b, to]) + wide(rc[k, h, a, b, to])
                        + wide(rn[k, h, b, to]) + wide(rf[k, h, to])
                    )
                    arrivals[tag, 3, k, h, i] = send(
                        acc.at[k, h, c, a, b, to], rz.at[k, h, i - 1], along_z[i - 1]
                    )

        def finish(k):
            totals = []
            for h in range(2):
                a, b = near[h], far[h]
                total = wide(acc[k, h, c, a, b, z]) + wide(rc[k, h, a, b, z])
                total += wide(rn[k, h, b, z]) + wide(rf[k, h, z])
                for i in range(1, depth):
                    arrivals[tag, 3, k, h, i].wait_recv()
                    total += wide(rz[k, h, i - 1])
                totals.append(total * scale)
            return soften_pair(*totals)

        return core_send, near_send, far_send, z_send, finish

    core_send, near_send, far_send, z_send, finish = reduce_stages(
        1, sums, from_core, from_near, from_far, from_z
    )

    def product(k):
        for h in range(2):
            loads["first", k, h].wait()
        def half(part):
            @pl.loop(0, depth)
            def _(zz):
                for yy in range(2):
                    for xx in range(2):
                        start = pl.multiple_of((((zz * 2 + part) * 2 + yy) * 2 + xx) * strip, strip)
                        field = field_at(start, strip, k)
                        for h in range(2):
                            at = h * cells + k * width
                            value = wide(first[pl.ds(start, strip), at : at + width]) * field
                            a, b = ((xx, yy), (yy, xx))[h]
                            sums[k, h, part, a, b, zz] = low(value)
        half(1 - c)
        core_send(k)
        half(c)

    def first_mask(k):
        real, imag = finish(k)
        for h, value in enumerate((real, imag)):
            at = h * cells + k * width
            out_one[:, at : at + width] = value
            a, b = near[h], far[h]
            mask[k, h, c, a, b, z] = low(value)
            for i in range(1, depth):
                arrivals["g", 0, k, h, i] = send(
                    mask.at[k, h, c, a, b, z], mask.at[k, h, c, a, b, z], along_z[i - 1]
                )

    def gather_far(k):
        for h in range(2):
            for i in range(1, depth):
                arrivals["g", 0, k, h, i].wait_recv()
            at = mask.at[k, h, c, near[h], far[h]]
            arrivals["g", 1, k, h] = send(at, at, far_dev[h])

    def gather_near(k):
        for h in range(2):
            arrivals["g", 1, k, h].wait_recv()
            at = mask.at[k, h, c, near[h]]
            arrivals["g", 2, k, h] = send(at, at, near_dev[h])

    def gather_core(k):
        for h in range(2):
            arrivals["g", 2, k, h].wait_recv()
            at = mask.at[k, h, c]
            arrivals["g", 3, k, h] = send(at, at, sibling)

    def gather_done(k):
        for h in range(2):
            arrivals["g", 3, k, h].wait_recv()
        piece = pl.ds(k % pieces * width, width)

        @pl.loop(0, depth)
        def _(zz):
            for cc in range(2):
                for yy in range(2):
                    for xx in range(2):
                        start = pl.multiple_of((((zz * 2 + cc) * 2 + yy) * 2 + xx) * strip, strip)
                        field = field_at(start, strip, k)
                        for h in range(2):
                            a, b = ((xx, yy), (yy, xx))[h]
                            applied[k // pieces, h, pl.ds(start, strip), piece] = low(
                                wide(mask[k, h, cc, a, b, zz]) * field
                            )

    def schedule(stages, keys, between=None):
        order = sorted(
            (keys[s][0] + keys[s][1] * k, -s, k) for s in range(len(stages)) for k in range(chunks)
        )
        waiting, done = [(-s, k) for _, s, k in order], []
        while waiting:
            s, k = next((s, k) for s, k in waiting if s == 0 or (s - 1, k) in done)
            waiting.remove((s, k))
            done.append((s, k))
            if between and len(done) == 2 * chunks:
                between()
            stages[s](k)

    def build_tables():
        one = lax.broadcasted_iota(jnp.int32, (quarter, quarter), 0)
        two = lax.broadcasted_iota(jnp.int32, (quarter, quarter), 1)
        square = lax.rem((one - two) * (one - two), 2 * cells)
        phase = square.astype(jnp.float32) * (math.pi / cells)
        factor = cells ** (-0.5)
        real, imag = wide(low(jnp.cos(phase) * factor)), wide(low(jnp.sin(phase) * factor))
        for table, diff, sign in ((table_col, two - one, 1.0), (table_row, one - two, -1.0)):
            for r in range(4):
                keep = (diff & 3) == r
                rr = jnp.where(keep, real, 0.0)
                ii = jnp.where(keep, imag, 0.0)
                table[r, :quarter, :quarter] = low(rr)
                table[r, quarter:, quarter:] = low(rr)
                table[r, :quarter, quarter:] = low(sign * ii)
                table[r, quarter:, :quarter] = low(-sign * ii)

    schedule(
        (product, near_send, far_send, z_send, first_mask, gather_far, gather_near, gather_core, gather_done),
        KEYS, build_tables,
    )

    @pl.loop(0, depth)
    def _(zz):
        start = pl.multiple_of(zz * block, block)
        sides = [
            [wide(applied[q, h, pl.ds(start, block), :]) for q in range(4)] for h in range(2)
        ]
        outs = []
        for r, pair in enumerate(four_sums(sides[0], sides[1], -1.0)):
            both = low(jnp.concatenate(pair, axis=1))
            outs.append(jnp.dot(both, table_col[r], preferred_element_type=jnp.float32))
        done = four_sums([o[:, :quarter] for o in outs], [o[:, quarter:] for o in outs], 1.0)
        for p in range(4):
            for h in range(2):
                spread[p, h, pl.ds(start, block), :] = low(done[p][h])

    core_send2, near_send2, far_send2, z_send2, finish2 = reduce_stages(
        2, sums2, from_core2, from_near2, from_far2, from_z2
    )

    def arrive(k):
        if k == 0:
            loads["second"].wait()
        piece = pl.ds(k % pieces * width, width)
        sides = [
            [wide(spread[k // pieces, h, q * quarter : (q + 1) * quarter, piece]) for q in range(4)]
            for h in range(2)
        ]
        outs = []
        for r, pair in enumerate(four_sums(sides[0], sides[1], -1.0)):
            both = low(jnp.concatenate(pair, axis=0))
            outs.append(jnp.dot(table_row[r], both, preferred_element_type=jnp.float32))
        done = four_sums([o[:quarter] for o in outs], [o[quarter:] for o in outs], 1.0)
        for p in range(4):
            rows = slice(p * quarter, (p + 1) * quarter)
            back_real = wide(second[rows, k * width : (k + 1) * width])
            back_imag = wide(second[rows, cells + k * width : cells + (k + 1) * width])
            arr_real, arr_imag = done[p]
            terms = (
                back_real * arr_real + back_imag * arr_imag,
                back_imag * arr_real - back_real * arr_imag,
            )
            for h in range(2):
                value = low(terms[h])
                for n in range(quarter // strip):
                    number = p * (quarter // strip) + n
                    xx, yy, cc, zz = number % 2, number // 2 % 2, number // 4 % 2, number // 8
                    a, b = ((xx, yy), (yy, xx))[h]
                    sums2[k, h, cc, a, b, zz] = value[n * strip : (n + 1) * strip]
        core_send2(k)

    def second_mask(k):
        real, imag = finish2(k)
        out_two[:, k * width : (k + 1) * width] = real
        out_two[:, cells + k * width : cells + (k + 1) * width] = imag

    schedule((arrive, near_send2, far_send2, z_send2, second_mask), KEYS_TWO)
    for copy in sent:
        copy.wait_send()


def hand_on_kernel(one_in, two_in, one_out, two_out):
    one_out[...] = one_in[...]
    two_out[...] = two_in[...]


def sweep_call(modes, back_first, back_second, devices, depth, scale):
    cells = back_first.shape[0]
    strip, width, chunks = cells // devices, cells // CHUNKS, CHUNKS
    low = jnp.bfloat16
    tail = (strip, width)
    received = [
        pltpu.VMEM((chunks, 2, 2, 2, depth) + tail, low),
        pltpu.VMEM((chunks, 2, 2, depth) + tail, low),
        pltpu.VMEM((chunks, 2, depth) + tail, low),
        pltpu.VMEM((chunks, 2, depth - 1) + tail, low),
    ]
    whole = pltpu.VMEM((chunks, 2, 2, 2, 2, depth) + tail, low)
    table = pltpu.VMEM((4, cells // 2, cells // 2), low)
    copies = 3 * chunks * 2 * (3 + depth - 1)
    vmem = pl.BlockSpec(memory_space=pltpu.VMEM)
    hbm = pl.BlockSpec(memory_space=pl.ANY)
    out = jax.ShapeDtypeStruct((strip, 2 * cells), jnp.float32)
    swept = pl.pallas_call(
        functools.partial(sweep_kernel, depth, scale),
        out_shape=(out, out),
        in_specs=[vmem, hbm, hbm],
        out_specs=(vmem, vmem),
        scratch_shapes=[pltpu.VMEM((cells, 2 * cells), low)] * 2
        + [whole] + received + [whole] + received
        + [whole] + [pltpu.VMEM((4, 2, cells, cells // 4), low)] * 2 + [table, table]
        + [pltpu.VMEM((cells, 128), jnp.float32), pltpu.VMEM((1, cells), jnp.float32)]
        + [
            pltpu.SemaphoreType.DMA((2 * chunks + 1,)),
            pltpu.SemaphoreType.DMA((copies,)),
            pltpu.SemaphoreType.DMA((copies,)),
        ],
        compiler_params=pltpu.CompilerParams(
            collective_id=0, has_side_effects=True, vmem_limit_bytes=60 * 1024 * 1024
        ),
        name="sweep",
    )(modes, back_first, back_second)
    return pl.pallas_call(
        hand_on_kernel,
        out_shape=(out, out),
        in_specs=[vmem, vmem],
        out_specs=(vmem, vmem),
        compiler_params=pltpu.CompilerParams(vmem_limit_bytes=63 * 1024 * 1024),
        name="hand_on",
    )(*swept)


def body(in_modes, back_first, back_second):
    mode_dev = in_modes.shape[0]
    cells = back_first.shape[1]
    axes = ("mgroup", "msub")
    devices_all = lax.axis_size("mgroup") * lax.axis_size("msub")
    scale_all = float(mode_dev * devices_all) ** (-0.5)
    depth = lax.axis_size("mgroup") // 2
    if mode_dev == 1 and lax.axis_size("msub") == 4 and depth == 4 and cells % (16 * devices_all) == cells % (128 * CHUNKS) == 0:
        return sweep_call(
            in_modes, back_first[0], back_second[0], devices_all, depth, scale_all
        )
    herm_table = hermite_table(grid_points(cells))
    row_funcs = pick_funcs(in_modes[:, 0], herm_table)
    col_funcs = pick_funcs(in_modes[:, 1], herm_table)
    fields = (row_funcs[:, :, None] * col_funcs[:, None, :]).astype(jnp.bfloat16)
    table = residue_chirp(cells)
    first = intersection_first(back_first, fields).astype(jnp.bfloat16)
    summed = lax.psum_scatter(first, axes, scatter_dimension=0, tiled=True)
    mask_first = soften(summed.astype(jnp.float32) * scale_all)
    full_mask = lax.all_gather(mask_first.astype(jnp.bfloat16), axes, axis=0, tiled=True)
    full_mask = full_mask.astype(jnp.float32)
    real_part, imag_part = 0.0, 0.0
    for mode in range(mode_dev):
        field = fields[mode].astype(jnp.float32)
        real = (full_mask[:, :cells] * field).astype(jnp.bfloat16).astype(jnp.float32)
        imag = (full_mask[:, cells:] * field).astype(jnp.bfloat16).astype(jnp.float32)
        arr_real, arr_imag = propagate_down(*propagate_columns(real, imag, table), table)
        back = back_second[mode].astype(jnp.float32)
        back_real, back_imag = back[:, :cells], back[:, cells:]
        real_part += back_real * arr_real + back_imag * arr_imag
        imag_part += back_imag * arr_real - back_real * arr_imag
    second = jnp.concatenate([real_part, imag_part], axis=1).astype(jnp.bfloat16)
    summed_two = lax.psum_scatter(second, axes, scatter_dimension=0, tiled=True)
    mask_second = soften(summed_two.astype(jnp.float32) * scale_all)
    return (mask_first, mask_second)


def solution(mesh):
    placed = (
        P(("mgroup", "msub"), None),
        P(("mgroup", "msub"), None, None),
        P(("mgroup", "msub"), None, None),
    )
    return jax.shard_map(
        body,
        mesh=mesh,
        in_specs=placed,
        out_specs=(P(("mgroup", "msub"), None), P(("mgroup", "msub"), None)),
        check_vma=False,
    )
```

```python
import functools
import math

import jax
import jax.numpy as jnp
from jax import lax
from jax.experimental import pallas as pl
from jax.experimental.pallas import tpu as pltpu
from jax.sharding import PartitionSpec as P

ORDERS = 32


span_width = 24.0


def grid_points(cells):
    index = jnp.arange(cells, dtype=jnp.float32)
    return (index - cells / 2 + 0.5) * (span_width / cells)


def hermite_table(points):
    before = jnp.zeros_like(points)
    current = math.pi ** (-0.25) * jnp.exp(-0.5 * points * points)
    collected = []
    for order in range(ORDERS):
        collected.append(current)
        following = (
            math.sqrt(2.0 / (order + 1)) * points * current
            - math.sqrt(order / (order + 1.0)) * before
        )
        before, current = (current, following)
    return jnp.stack(collected, axis=0)


def chirp_parts(cells):
    index = jnp.arange(cells, dtype=jnp.int32)
    offset = index[:, None] - index[None, :]
    square = offset * offset % (2 * cells)
    phase = square.astype(jnp.float32) * (math.pi / cells)
    factor = cells ** (-0.5)
    return (
        (jnp.cos(phase) * factor).astype(jnp.bfloat16),
        (jnp.sin(phase) * factor).astype(jnp.bfloat16),
    )


def soften(intersection):
    half = intersection.shape[-1] // 2
    real_part = intersection[..., :half]
    imag_part = intersection[..., half:]
    denom = jnp.sqrt(real_part * real_part + imag_part * imag_part + 1.0)
    return intersection / jnp.concatenate([denom, denom], axis=-1)


def pick_funcs(orders, herm_table):
    one_hot = (orders[:, None] == jnp.arange(herm_table.shape[0], dtype=jnp.int32)[None, :]).astype(
        jnp.float32
    )
    return jnp.dot(one_hot, herm_table, precision=lax.Precision.HIGHEST)


def intersection_first(back_rows, field_rows):
    widened = field_rows.astype(jnp.float32)
    tiled = jnp.concatenate([widened, widened], axis=2)
    return jnp.sum(back_rows.astype(jnp.float32) * tiled, axis=0)


def residue_chirp(cells):
    block = cells // 4
    chirp_real, chirp_imag = chirp_parts(cells)
    index = jnp.arange(block, dtype=jnp.int32)
    residue = (index[None, :] - index[:, None]) % 4
    keep = residue[None] == jnp.arange(4, dtype=jnp.int32)[:, None, None]
    real = jnp.where(keep, chirp_real[None, :block, :block], 0)
    imag = jnp.where(keep, chirp_imag[None, :block, :block], 0)
    return jnp.concatenate(
        [jnp.concatenate([real, imag], axis=2), jnp.concatenate([-imag, real], axis=2)], axis=1
    )


def four_sums(real, imag, sign):
    even_r, even_i = real[0] + real[2], imag[0] + imag[2]
    odd_r, odd_i = real[1] + real[3], imag[1] + imag[3]
    low_r, low_i = real[0] - real[2], imag[0] - imag[2]
    one, three = (1, 3) if sign > 0 else (3, 1)
    top_r, top_i = real[one] - real[three], imag[one] - imag[three]
    return (
        (even_r + odd_r, even_i + odd_i),
        (low_r - top_i, low_i + top_r),
        (even_r - odd_r, even_i - odd_i),
        (low_r + top_i, low_i - top_r),
    )


def split_four(array, axis):
    return jnp.split(array, 4, axis=axis)


def propagate_columns(real, imag, table):
    block = real.shape[1] // 4
    parts = four_sums(split_four(real, 1), split_four(imag, 1), -1.0)
    outs = []
    for r in range(4):
        both = jnp.concatenate(parts[r], axis=1).astype(jnp.bfloat16)
        outs.append(jnp.dot(both, table[r], preferred_element_type=jnp.float32))
    sums = four_sums([o[:, :block] for o in outs], [o[:, block:] for o in outs], 1.0)
    return [jnp.concatenate([s[k] for s in sums], axis=1).astype(jnp.bfloat16) for k in (0, 1)]


def propagate_down(real, imag, table):
    block = real.shape[0] // 4
    parts = four_sums(
        split_four(real.astype(jnp.float32), 0), split_four(imag.astype(jnp.float32), 0), -1.0
    )
    outs = []
    for r in range(4):
        both = jnp.concatenate(parts[r], axis=0).astype(jnp.bfloat16)
        outs.append(jnp.dot(table[r].T, both, preferred_element_type=jnp.float32))
    sums = four_sums([o[:block] for o in outs], [o[block:] for o in outs], 1.0)
    return [jnp.concatenate([s[k] for s in sums], axis=0) for k in (0, 1)]


MESH = pl.DeviceIdType.MESH
CHUNKS = 8
KEYS = (
    (0.3, 0.7), (1.1, 0.9), (2.8, 0.9), (3.7, 1.0), (5.2, 1.0),
    (7.0, 0.9), (8.9, 0.8), (11.5, 0.8), (12.7, 1.1),
)
KEYS_TWO = ((0.0, 0.5), (1.4, 0.5), (3.3, 0.3), (3.9, 0.3), (22.7, 6.4))


def sweep_kernel(
    depth, scale,
    modes_ref, first_hbm, second_hbm, out_one, out_two,
    first, second, sums, from_core, from_near, from_far, from_z,
    sums2, from_core2, from_near2, from_far2, from_z2,
    mask, applied, spread, partial, table_col, table_row, row_ref, col_ref, local_sem, send_sem, recv_sem,
):
    cells = first.shape[0]
    chunks, strip, width = sums.shape[0], sums.shape[6], sums.shape[7]
    block = cells // depth
    quarter = cells // 4
    pieces = quarter // width
    column = [k % 4 * quarter + k // 4 * width for k in range(chunks)]
    group, sub = lax.axis_index("mgroup"), lax.axis_index("msub")
    z, c = group // 2, group % 2
    y, x = sub // 2, sub % 2
    sibling = (z * 2 + 1 - c, sub)
    across_x = (group, y * 2 + 1 - x)
    across_y = (group, (1 - y) * 2 + x)
    along_z = [(lax.rem(z + i, depth) * 2 + c, sub) for i in range(1, depth)]
    near, far = (x, y), (y, x)
    near_dev, far_dev = (across_x, across_y), (across_y, across_x)

    barrier = pltpu.get_barrier_semaphore()
    for peer in [sibling, across_x, across_y] + along_z:
        pl.semaphore_signal(barrier, inc=1, device_id=peer, device_id_type=MESH)

    loads = {}
    def load(name, src, dst):
        copy = pltpu.make_async_copy(src, dst, local_sem.at[len(loads)])
        copy.start()
        loads[name] = copy
    for k in range(chunks):
        for h in range(2):
            at = pl.ds(h * cells + column[k], width)
            load(("first", k, h), first_hbm.at[:, at], first.at[:, at])
    load("second", second_hbm, second)

    lanes = row_ref.shape[1]
    index = lax.broadcasted_iota(jnp.int32, (8, cells), 1).astype(jnp.float32)
    points = (index - cells / 2 + 0.5) * (span_width / cells)
    orders = modes_ref[...]
    row_order, col_order = orders[:, 0:1], orders[:, 1:2]
    before, current = jnp.zeros_like(points), math.pi ** (-0.25) * jnp.exp(-0.5 * points * points)
    row_func, col_func = before, before
    for order in range(ORDERS):
        row_func = jnp.where(row_order == order, current, row_func)
        col_func = jnp.where(col_order == order, current, col_func)
        before, current = current, (
            math.sqrt(2.0 / (order + 1)) * points * current
            - math.sqrt(order / (order + 1.0)) * before
        )
    col_ref[...] = col_func[:1]
    row_ref[...] = jnp.broadcast_to(row_func[:1], (lanes, cells)).T

    sent = []
    def send(src, dst, peer):
        at = len(sent)
        copy = pltpu.make_async_remote_copy(
            src_ref=src, dst_ref=dst, send_sem=send_sem.at[at], recv_sem=recv_sem.at[at],
            device_id=peer, device_id_type=MESH,
        )
        copy.start()
        sent.append(copy)
        return copy

    def field_at(start, rows, k):
        col = col_ref[:, column[k] : column[k] + width]
        row = jnp.concatenate([row_ref[pl.ds(start, rows), :]] * (width // lanes), axis=1)
        return (row * col).astype(jnp.bfloat16)

    def soften_pair(real, imag):
        factor = lax.rsqrt(real * real + imag * imag + 1.0)
        return real * factor, imag * factor

    wide = lambda value: value.astype(jnp.float32)
    low = lambda value: value.astype(jnp.bfloat16)
    arrivals = {}

    def reduce_stages(tag, acc, rc, rn, rf, rz):
        def core_send(k):
            arrivals[tag, 0, k] = send(acc.at[k, 1 - c], rc.at[k], sibling)

        def near_send(k):
            arrivals[tag, 0, k].wait_recv()
            for h in range(2):
                a = 1 - near[h]
                acc[k, c, h, a] = acc[k, c, h, a] + rc[k, h, a]
                arrivals[tag, 1, k, h] = send(acc.at[k, c, h, a], rn.at[k, h], near_dev[h])

        def far_send(k):
            for h in range(2):
                arrivals[tag, 1, k, h].wait_recv()
                a, b = near[h], 1 - far[h]
                acc[k, c, h, a, b] = low(
                    wide(acc[k, c, h, a, b]) + wide(rc[k, h, a, b]) + wide(rn[k, h, b])
                )
                arrivals[tag, 2, k, h] = send(acc.at[k, c, h, a, b], rf.at[k, h], far_dev[h])

        def z_send(k):
            for h in range(2):
                arrivals[tag, 2, k, h].wait_recv()
                a, b = near[h], far[h]
                for i in range(1, depth):
                    to = lax.rem(z + i, depth)
                    acc[k, c, h, a, b, to] = low(
                        wide(acc[k, c, h, a, b, to]) + wide(rc[k, h, a, b, to])
                        + wide(rn[k, h, b, to]) + wide(rf[k, h, to])
                    )
                    arrivals[tag, 3, k, h, i] = send(
                        acc.at[k, c, h, a, b, to], rz.at[k, h, i - 1], along_z[i - 1]
                    )

        def finish(k):
            totals = []
            for h in range(2):
                a, b = near[h], far[h]
                total = wide(acc[k, c, h, a, b, z]) + wide(rc[k, h, a, b, z])
                total += wide(rn[k, h, b, z]) + wide(rf[k, h, z])
                for i in range(1, depth):
                    arrivals[tag, 3, k, h, i].wait_recv()
                    total += wide(rz[k, h, i - 1])
                totals.append(total * scale)
            return soften_pair(*totals)

        return core_send, near_send, far_send, z_send, finish

    core_send, near_send, far_send, z_send, finish = reduce_stages(
        1, sums, from_core, from_near, from_far, from_z
    )

    def product(k):
        for h in range(2):
            loads["first", k, h].wait()
        def half(part):
            @pl.loop(0, depth)
            def _(zz):
                for yy in range(2):
                    for xx in range(2):
                        start = pl.multiple_of((((zz * 2 + part) * 2 + yy) * 2 + xx) * strip, strip)
                        field = field_at(start, strip, k)
                        for h in range(2):
                            at = h * cells + column[k]
                            a, b = ((xx, yy), (yy, xx))[h]
                            sums[k, part, h, a, b, zz] = first[pl.ds(start, strip), at : at + width] * field
        half(1 - c)
        if k == 0:
            pl.semaphore_wait(barrier, 2 + depth)
        core_send(k)
        half(c)

    def first_mask(k):
        real, imag = finish(k)
        for h, value in enumerate((real, imag)):
            at = h * cells + column[k]
            out_one[:, at : at + width] = value
            a, b = near[h], far[h]
            mask[k, c, h, a, b, z] = low(value)
            for i in range(1, depth):
                arrivals["g", 0, k, h, i] = send(
                    mask.at[k, c, h, a, b, z], mask.at[k, c, h, a, b, z], along_z[i - 1]
                )

    def gather_far(k):
        for h in range(2):
            for i in range(1, depth):
                arrivals["g", 0, k, h, i].wait_recv()
            at = mask.at[k, c, h, near[h], far[h]]
            arrivals["g", 1, k, h] = send(at, at, far_dev[h])

    def gather_near(k):
        for h in range(2):
            arrivals["g", 1, k, h].wait_recv()
            at = mask.at[k, c, h, near[h]]
            arrivals["g", 2, k, h] = send(at, at, near_dev[h])

    def gather_core(k):
        for h in range(2):
            arrivals["g", 2, k, h].wait_recv()
        at = mask.at[k, c]
        arrivals["g", 3, k] = send(at, at, sibling)

    def gather_done(k):
        arrivals["g", 3, k].wait_recv()

        @pl.loop(0, depth)
        def _(zz):
            for cc in range(2):
                for yy in range(2):
                    for xx in range(2):
                        start = pl.multiple_of((((zz * 2 + cc) * 2 + yy) * 2 + xx) * strip, strip)
                        field = field_at(start, strip, k)
                        for h in range(2):
                            a, b = ((xx, yy), (yy, xx))[h]
                            applied[k, h, pl.ds(start, strip), :] = mask[k, cc, h, a, b, zz] * field

    def columns_part(zz, part):
        start = pl.multiple_of(zz * block, block)
        sides = [
            [applied[part * 4 + q, h, pl.ds(start, block), :] for q in range(4)] for h in range(2)
        ]
        for r, pair in enumerate(four_sums(sides[0], sides[1], -1)):
            both = jnp.concatenate(pair, axis=1)
            rows = slice(part * 2 * width, (part + 1) * 2 * width)
            out = jnp.dot(both, table_col[r, rows], preferred_element_type=jnp.float32)
            if part > 0:
                out += partial[r, pl.ds(start, block), :]
            if part < pieces - 1:
                partial[r, pl.ds(start, block), :] = out
            else:
                yield out

    def early_columns(k):
        gather_done(k)
        for zz in range(depth):
            part, last = divmod(k - zz - 3, 4)
            if last == 0 and 0 <= part < pieces - 1:
                for _ in columns_part(zz, part):
                    pass

    def schedule(stages, keys, between=None):
        order = sorted(
            (keys[s][0] + keys[s][1] * k, -s, k) for s in range(len(stages)) for k in range(chunks)
        )
        waiting, done = [(-s, k) for _, s, k in order], []
        while waiting:
            s, k = next((s, k) for s, k in waiting if s == 0 or (s - 1, k) in done)
            waiting.remove((s, k))
            done.append((s, k))
            if between and len(done) == 2 * chunks:
                between()
            stages[s](k)

    def build_tables():
        one = lax.broadcasted_iota(jnp.int32, (quarter, quarter), 0)
        two = lax.broadcasted_iota(jnp.int32, (quarter, quarter), 1)
        square = lax.rem((one - two) * (one - two), 2 * cells)
        phase = square.astype(jnp.float32) * (math.pi / cells)
        factor = cells ** (-0.5)
        real, imag = wide(low(jnp.cos(phase) * factor)), wide(low(jnp.sin(phase) * factor))
        for r in range(4):
            keep = ((two - one) & 3) == r
            rr, ii = low(jnp.where(keep, real, 0.0)), low(jnp.where(keep, imag, 0.0))
            for n in range(pieces):
                rows = slice(n * width, (n + 1) * width)
                to = 2 * n * width
                table_col[r, to : to + width, :quarter] = rr[rows]
                table_col[r, to : to + width, quarter:] = ii[rows]
                table_col[r, to + width : to + 2 * width, :quarter] = -ii[rows]
                table_col[r, to + width : to + 2 * width, quarter:] = rr[rows]
            keep = ((one - two) & 3) == r
            rr, ii = low(jnp.where(keep, real, 0.0)), low(jnp.where(keep, imag, 0.0))
            table_row[r, :quarter, :quarter] = rr
            table_row[r, quarter:, quarter:] = rr
            table_row[r, :quarter, quarter:] = -ii
            table_row[r, quarter:, :quarter] = ii

    schedule(
        (product, near_send, far_send, z_send, first_mask, gather_far, gather_near, gather_core, early_columns),
        KEYS, build_tables,
    )

    @pl.loop(0, depth)
    def _(zz):
        start = pl.multiple_of(zz * block, block)
        outs = list(columns_part(zz, pieces - 1))
        done = four_sums([o[:, :quarter] for o in outs], [o[:, quarter:] for o in outs], 1.0)
        for p in range(4):
            for h in range(2):
                spread[p, h, pl.ds(start, block), :] = low(done[p][h])

    core_send2, near_send2, far_send2, z_send2, finish2 = reduce_stages(
        2, sums2, from_core2, from_near2, from_far2, from_z2
    )

    def arrive(k):
        if k == 0:
            loads["second"].wait()
        piece = pl.ds(k // 4 * width, width)
        sides = [
            [spread[k % 4, h, q * quarter : (q + 1) * quarter, piece] for q in range(4)]
            for h in range(2)
        ]
        outs = []
        for r, pair in enumerate(four_sums(sides[0], sides[1], -1)):
            both = jnp.concatenate(pair, axis=0)
            outs.append(jnp.dot(table_row[r], both, preferred_element_type=jnp.float32))
        done = four_sums([o[:quarter] for o in outs], [o[quarter:] for o in outs], 1.0)
        for p in range(4):
            rows = slice(p * quarter, (p + 1) * quarter)
            back_real = wide(second[rows, column[k] : column[k] + width])
            back_imag = wide(second[rows, cells + column[k] : cells + column[k] + width])
            arr_real, arr_imag = done[p]
            terms = (
                back_real * arr_real + back_imag * arr_imag,
                back_imag * arr_real - back_real * arr_imag,
            )
            for h in range(2):
                value = low(terms[h])
                for n in range(quarter // strip):
                    number = p * (quarter // strip) + n
                    xx, yy, cc, zz = number % 2, number // 2 % 2, number // 4 % 2, number // 8
                    a, b = ((xx, yy), (yy, xx))[h]
                    sums2[k, cc, h, a, b, zz] = value[n * strip : (n + 1) * strip]
        core_send2(k)

    def second_mask(k):
        real, imag = finish2(k)
        out_two[:, column[k] : column[k] + width] = real
        out_two[:, cells + column[k] : cells + column[k] + width] = imag

    schedule((arrive, near_send2, far_send2, z_send2, second_mask), KEYS_TWO)
    for copy in sent:
        copy.wait_send()


def hand_on_kernel(one_in, two_in, one_out, two_out):
    one_out[...] = one_in[...]
    two_out[...] = two_in[...]


def sweep_call(modes, back_first, back_second, devices, depth, scale):
    cells = back_first.shape[0]
    strip, width, chunks = cells // devices, cells // CHUNKS, CHUNKS
    low = jnp.bfloat16
    tail = (strip, width)
    received = [
        pltpu.VMEM((chunks, 2, 2, 2, depth) + tail, low),
        pltpu.VMEM((chunks, 2, 2, depth) + tail, low),
        pltpu.VMEM((chunks, 2, depth) + tail, low),
        pltpu.VMEM((chunks, 2, depth - 1) + tail, low),
    ]
    whole = pltpu.VMEM((chunks, 2, 2, 2, 2, depth) + tail, low)
    table = pltpu.VMEM((4, cells // 2, cells // 2), low)
    copies = 3 * chunks * 2 * (3 + depth - 1)
    vmem = pl.BlockSpec(memory_space=pltpu.VMEM)
    hbm = pl.BlockSpec(memory_space=pl.ANY)
    out = jax.ShapeDtypeStruct((strip, 2 * cells), jnp.float32)
    swept = pl.pallas_call(
        functools.partial(sweep_kernel, depth, scale),
        out_shape=(out, out),
        in_specs=[vmem, hbm, hbm],
        out_specs=(vmem, vmem),
        scratch_shapes=[pltpu.VMEM((cells, 2 * cells), low)] * 2
        + [whole] + received + [whole] + received
        + [whole] + [pltpu.VMEM((chunks, 2, cells, width), low), pltpu.VMEM((4, 2, cells, cells // 4), low)]
        + [pltpu.VMEM((4, cells, cells // 2), jnp.float32), table, table]
        + [pltpu.VMEM((cells, 128), jnp.float32), pltpu.VMEM((1, cells), jnp.float32)]
        + [
            pltpu.SemaphoreType.DMA((2 * chunks + 1,)),
            pltpu.SemaphoreType.DMA((copies,)),
            pltpu.SemaphoreType.DMA((copies,)),
        ],
        compiler_params=pltpu.CompilerParams(
            collective_id=0, has_side_effects=True, vmem_limit_bytes=60 * 1024 * 1024
        ),
        name="sweep",
    )(modes, back_first, back_second)
    return pl.pallas_call(
        hand_on_kernel,
        out_shape=(out, out),
        in_specs=[vmem, vmem],
        out_specs=(vmem, vmem),
        compiler_params=pltpu.CompilerParams(vmem_limit_bytes=63 * 1024 * 1024),
        name="hand_on",
    )(*swept)


def body(in_modes, back_first, back_second):
    mode_dev = in_modes.shape[0]
    cells = back_first.shape[1]
    axes = ("mgroup", "msub")
    devices_all = lax.axis_size("mgroup") * lax.axis_size("msub")
    scale_all = float(mode_dev * devices_all) ** (-0.5)
    depth = lax.axis_size("mgroup") // 2
    if mode_dev == 1 and lax.axis_size("msub") == 4 and depth == 4 and cells % (16 * devices_all) == cells % (128 * CHUNKS) == 0:
        return sweep_call(
            in_modes, back_first[0], back_second[0], devices_all, depth, scale_all
        )
    herm_table = hermite_table(grid_points(cells))
    row_funcs = pick_funcs(in_modes[:, 0], herm_table)
    col_funcs = pick_funcs(in_modes[:, 1], herm_table)
    fields = (row_funcs[:, :, None] * col_funcs[:, None, :]).astype(jnp.bfloat16)
    table = residue_chirp(cells)
    first = intersection_first(back_first, fields).astype(jnp.bfloat16)
    summed = lax.psum_scatter(first, axes, scatter_dimension=0, tiled=True)
    mask_first = soften(summed.astype(jnp.float32) * scale_all)
    full_mask = lax.all_gather(mask_first.astype(jnp.bfloat16), axes, axis=0, tiled=True)
    full_mask = full_mask.astype(jnp.float32)
    real_part, imag_part = 0.0, 0.0
    for mode in range(mode_dev):
        field = fields[mode].astype(jnp.float32)
        real = (full_mask[:, :cells] * field).astype(jnp.bfloat16).astype(jnp.float32)
        imag = (full_mask[:, cells:] * field).astype(jnp.bfloat16).astype(jnp.float32)
        arr_real, arr_imag = propagate_down(*propagate_columns(real, imag, table), table)
        back = back_second[mode].astype(jnp.float32)
        back_real, back_imag = back[:, :cells], back[:, cells:]
        real_part += back_real * arr_real + back_imag * arr_imag
        imag_part += back_imag * arr_real - back_real * arr_imag
    second = jnp.concatenate([real_part, imag_part], axis=1).astype(jnp.bfloat16)
    summed_two = lax.psum_scatter(second, axes, scatter_dimension=0, tiled=True)
    mask_second = soften(summed_two.astype(jnp.float32) * scale_all)
    return (mask_first, mask_second)


def solution(mesh):
    placed = (
        P(("mgroup", "msub"), None),
        P(("mgroup", "msub"), None, None),
        P(("mgroup", "msub"), None, None),
    )
    return jax.shard_map(
        body,
        mesh=mesh,
        in_specs=placed,
        out_specs=(P(("mgroup", "msub"), None), P(("mgroup", "msub"), None)),
        check_vma=False,
    )
```

```python
import functools
import math

import jax
import jax.numpy as jnp
from jax import lax
from jax.experimental import pallas as pl
from jax.experimental.pallas import tpu as pltpu
from jax.sharding import PartitionSpec as P

ORDERS = 32


span_width = 24.0


def grid_points(cells):
    index = jnp.arange(cells, dtype=jnp.float32)
    return (index - cells / 2 + 0.5) * (span_width / cells)


def hermite_table(points):
    before = jnp.zeros_like(points)
    current = math.pi ** (-0.25) * jnp.exp(-0.5 * points * points)
    collected = []
    for order in range(ORDERS):
        collected.append(current)
        following = (
            math.sqrt(2.0 / (order + 1)) * points * current
            - math.sqrt(order / (order + 1.0)) * before
        )
        before, current = (current, following)
    return jnp.stack(collected, axis=0)


def chirp_parts(cells):
    index = jnp.arange(cells, dtype=jnp.int32)
    offset = index[:, None] - index[None, :]
    square = offset * offset % (2 * cells)
    phase = square.astype(jnp.float32) * (math.pi / cells)
    factor = cells ** (-0.5)
    return (
        (jnp.cos(phase) * factor).astype(jnp.bfloat16),
        (jnp.sin(phase) * factor).astype(jnp.bfloat16),
    )


def soften(intersection):
    half = intersection.shape[-1] // 2
    real_part = intersection[..., :half]
    imag_part = intersection[..., half:]
    denom = jnp.sqrt(real_part * real_part + imag_part * imag_part + 1.0)
    return intersection / jnp.concatenate([denom, denom], axis=-1)


def pick_funcs(orders, herm_table):
    one_hot = (orders[:, None] == jnp.arange(herm_table.shape[0], dtype=jnp.int32)[None, :]).astype(
        jnp.float32
    )
    return jnp.dot(one_hot, herm_table, precision=lax.Precision.HIGHEST)


def intersection_first(back_rows, field_rows):
    widened = field_rows.astype(jnp.float32)
    tiled = jnp.concatenate([widened, widened], axis=2)
    return jnp.sum(back_rows.astype(jnp.float32) * tiled, axis=0)


def residue_chirp(cells):
    block = cells // 4
    chirp_real, chirp_imag = chirp_parts(cells)
    index = jnp.arange(block, dtype=jnp.int32)
    residue = (index[None, :] - index[:, None]) % 4
    keep = residue[None] == jnp.arange(4, dtype=jnp.int32)[:, None, None]
    real = jnp.where(keep, chirp_real[None, :block, :block], 0)
    imag = jnp.where(keep, chirp_imag[None, :block, :block], 0)
    return jnp.concatenate(
        [jnp.concatenate([real, imag], axis=2), jnp.concatenate([-imag, real], axis=2)], axis=1
    )


def four_sums(real, imag, sign):
    even_r, even_i = real[0] + real[2], imag[0] + imag[2]
    odd_r, odd_i = real[1] + real[3], imag[1] + imag[3]
    low_r, low_i = real[0] - real[2], imag[0] - imag[2]
    one, three = (1, 3) if sign > 0 else (3, 1)
    top_r, top_i = real[one] - real[three], imag[one] - imag[three]
    return (
        (even_r + odd_r, even_i + odd_i),
        (low_r - top_i, low_i + top_r),
        (even_r - odd_r, even_i - odd_i),
        (low_r + top_i, low_i - top_r),
    )


def split_four(array, axis):
    return jnp.split(array, 4, axis=axis)


def propagate_columns(real, imag, table):
    block = real.shape[1] // 4
    parts = four_sums(split_four(real, 1), split_four(imag, 1), -1.0)
    outs = []
    for r in range(4):
        both = jnp.concatenate(parts[r], axis=1).astype(jnp.bfloat16)
        outs.append(jnp.dot(both, table[r], preferred_element_type=jnp.float32))
    sums = four_sums([o[:, :block] for o in outs], [o[:, block:] for o in outs], 1.0)
    return [jnp.concatenate([s[k] for s in sums], axis=1).astype(jnp.bfloat16) for k in (0, 1)]


def propagate_down(real, imag, table):
    block = real.shape[0] // 4
    parts = four_sums(
        split_four(real.astype(jnp.float32), 0), split_four(imag.astype(jnp.float32), 0), -1.0
    )
    outs = []
    for r in range(4):
        both = jnp.concatenate(parts[r], axis=0).astype(jnp.bfloat16)
        outs.append(jnp.dot(table[r].T, both, preferred_element_type=jnp.float32))
    sums = four_sums([o[:block] for o in outs], [o[block:] for o in outs], 1.0)
    return [jnp.concatenate([s[k] for s in sums], axis=0) for k in (0, 1)]


MESH = pl.DeviceIdType.MESH
CHUNKS = 8
Z_FIRST = 2
KEYS = (
    (0.3, 0.7), (1.1, 0.9), (2.8, 0.9), (3.7, 1.0), (5.2, 1.0),
    (7.0, 0.9), (8.9, 0.8), (11.5, 0.8), (12.7, 1.1),
)
KEYS_TWO = ((0.0, 0.5), (1.4, 0.5), (3.3, 0.3), (3.9, 0.3), (22.7, 6.4))


def sweep_kernel(
    depth, scale,
    modes_ref, first_hbm, second_hbm, out_one, out_two,
    first, second, sums, from_core, from_near, from_far, from_z, z_first,
    sums2, from_core2, from_near2, from_far2, from_z2, z_first2,
    mask, applied, spread, partial, table_col, table_row, row_ref, col_ref, local_sem, send_sem, recv_sem,
):
    cells = first.shape[0]
    chunks, strip, width = sums.shape[0], sums.shape[6], sums.shape[7]
    block = cells // depth
    quarter = cells // 4
    pieces = quarter // width
    column = [k % 4 * quarter + k // 4 * width for k in range(chunks)]
    group, sub = lax.axis_index("mgroup"), lax.axis_index("msub")
    z, c = group // 2, group % 2
    y, x = sub // 2, sub % 2
    sibling = (z * 2 + 1 - c, sub)
    across_x = (group, y * 2 + 1 - x)
    across_y = (group, (1 - y) * 2 + x)
    along_z = [(lax.rem(z + i, depth) * 2 + c, sub) for i in range(1, depth)]
    near, far = (x, y), (y, x)
    near_dev, far_dev = (across_x, across_y), (across_y, across_x)

    barrier = pltpu.get_barrier_semaphore()
    for peer in [sibling, across_x, across_y] + along_z:
        pl.semaphore_signal(barrier, inc=1, device_id=peer, device_id_type=MESH)

    loads = {}
    def load(name, src, dst):
        copy = pltpu.make_async_copy(src, dst, local_sem.at[len(loads)])
        copy.start()
        loads[name] = copy
    for k in range(chunks):
        for h in range(2):
            at = pl.ds(h * cells + column[k], width)
            load(("first", k, h), first_hbm.at[:, at], first.at[:, at])
    load("second", second_hbm, second)

    lanes = row_ref.shape[1]
    index = lax.broadcasted_iota(jnp.int32, (8, cells), 1).astype(jnp.float32)
    points = (index - cells / 2 + 0.5) * (span_width / cells)
    orders = modes_ref[...]
    row_order, col_order = orders[:, 0:1], orders[:, 1:2]
    before, current = jnp.zeros_like(points), math.pi ** (-0.25) * jnp.exp(-0.5 * points * points)
    row_func, col_func = before, before
    for order in range(ORDERS):
        row_func = jnp.where(row_order == order, current, row_func)
        col_func = jnp.where(col_order == order, current, col_func)
        before, current = current, (
            math.sqrt(2.0 / (order + 1)) * points * current
            - math.sqrt(order / (order + 1.0)) * before
        )
    col_ref[...] = col_func[:1]
    row_ref[...] = jnp.broadcast_to(row_func[:1], (lanes, cells)).T

    sent = []
    def send(src, dst, peer):
        at = len(sent)
        copy = pltpu.make_async_remote_copy(
            src_ref=src, dst_ref=dst, send_sem=send_sem.at[at], recv_sem=recv_sem.at[at],
            device_id=peer, device_id_type=MESH,
        )
        copy.start()
        sent.append(copy)
        return copy

    def field_at(start, rows, k):
        col = col_ref[:, column[k] : column[k] + width]
        row = jnp.concatenate([row_ref[pl.ds(start, rows), :]] * (width // lanes), axis=1)
        return (row * col).astype(jnp.bfloat16)

    def soften_pair(real, imag):
        factor = lax.rsqrt(real * real + imag * imag + 1.0)
        return real * factor, imag * factor

    wide = lambda value: value.astype(jnp.float32)
    low = lambda value: value.astype(jnp.bfloat16)
    arrivals = {}

    def reduce_stages(tag, acc, rc, rn, rf, rz, zf):
        def core_send(k):
            arrivals[tag, 0, k] = send(acc.at[k, 1 - c], rc.at[k], sibling)

        def near_send(k):
            arrivals[tag, 0, k].wait_recv()
            for h in range(2):
                a = 1 - near[h]
                acc[k, c, h, a] = acc[k, c, h, a] + rc[k, h, a]
                arrivals[tag, 1, k, h] = send(acc.at[k, c, h, a], rn.at[k, h], near_dev[h])

        def far_send(k):
            for h in range(2):
                arrivals[tag, 1, k, h].wait_recv()
                a, b = near[h], 1 - far[h]
                acc[k, c, h, a, b] = low(
                    wide(acc[k, c, h, a, b]) + wide(rc[k, h, a, b]) + wide(rn[k, h, b])
                )
                arrivals[tag, 2, k, h] = send(acc.at[k, c, h, a, b], rf.at[k, h], far_dev[h])

        def z_send(k):
            for h in range(2):
                arrivals[tag, 2, k, h].wait_recv()
                a, b = near[h], far[h]
                for i in range(1, depth):
                    to = lax.rem(z + i, depth)
                    acc[k, c, h, a, b, to] = low(
                        wide(acc[k, c, h, a, b, to]) + wide(rc[k, h, a, b, to])
                        + wide(rn[k, h, b, to]) + wide(rf[k, h, to])
                    )
                    arrivals[tag, 3, k, h, i] = send(
                        acc.at[k, c, h, a, b, to], rz.at[k, h, i - 1], along_z[i - 1]
                    )

        def finish(k):
            totals = []
            for h in range(2):
                a, b = near[h], far[h]
                total = wide(acc[k, c, h, a, b, z]) + wide(rc[k, h, a, b, z])
                total += wide(rn[k, h, b, z]) + wide(rf[k, h, z])
                for i in range(1, depth):
                    arrivals[tag, 3, k, h, i].wait_recv()
                    total += wide(rz[k, h, i - 1])
                totals.append(total * scale)
            return soften_pair(*totals)

        def z_send_first(k):
            arrivals[tag, 0, k].wait_recv()
            for h in range(2):
                for i in range(1, depth):
                    to = lax.rem(z + i, depth)
                    acc[k, c, h, :, :, to] = acc[k, c, h, :, :, to] + rc[k, h, :, :, to]
                    arrivals[tag, 1, k, h, i] = send(
                        acc.at[k, c, h, :, :, to], zf.at[h, i - 1], along_z[i - 1]
                    )

        def z_total(k, h, a, b):
            total = wide(acc[k, c, h, a, b, z]) + wide(rc[k, h, a, b, z])
            for i in range(1, depth):
                total += wide(zf[h, i - 1, a, b])
            return total

        def near_send_second(k):
            for h in range(2):
                for i in range(1, depth):
                    arrivals[tag, 1, k, h, i].wait_recv()
                a = 1 - near[h]
                for b in range(2):
                    acc[k, c, h, a, b, z] = low(z_total(k, h, a, b))
                arrivals[tag, 2, k, h] = send(acc.at[k, c, h, a, :, z], rn.at[k, h, :, 0], near_dev[h])

        def far_send_last(k):
            for h in range(2):
                arrivals[tag, 2, k, h].wait_recv()
                a, b = near[h], 1 - far[h]
                acc[k, c, h, a, b, z] = low(z_total(k, h, a, b) + wide(rn[k, h, b, 0]))
                arrivals[tag, 3, k, h] = send(acc.at[k, c, h, a, b, z], rf.at[k, h, 0], far_dev[h])

        def finish_first(k):
            totals = []
            for h in range(2):
                a, b = near[h], far[h]
                arrivals[tag, 3, k, h].wait_recv()
                total = z_total(k, h, a, b) + wide(rn[k, h, b, 0]) + wide(rf[k, h, 0])
                totals.append(total * scale)
            return soften_pair(*totals)

        def choose(one, other):
            return lambda k: other(k) if k == Z_FIRST else one(k)

        return (
            core_send,
            choose(near_send, z_send_first),
            choose(far_send, near_send_second),
            choose(z_send, far_send_last),
            choose(finish, finish_first),
        )

    core_send, near_send, far_send, z_send, finish = reduce_stages(
        1, sums, from_core, from_near, from_far, from_z, z_first
    )

    def product(k):
        for h in range(2):
            loads["first", k, h].wait()
        def half(part):
            @pl.loop(0, depth)
            def _(zz):
                for yy in range(2):
                    for xx in range(2):
                        start = pl.multiple_of((((zz * 2 + part) * 2 + yy) * 2 + xx) * strip, strip)
                        field = field_at(start, strip, k)
                        for h in range(2):
                            at = h * cells + column[k]
                            a, b = ((xx, yy), (yy, xx))[h]
                            sums[k, part, h, a, b, zz] = first[pl.ds(start, strip), at : at + width] * field
        half(1 - c)
        if k == 0:
            pl.semaphore_wait(barrier, 2 + depth)
        core_send(k)
        half(c)

    def first_mask(k):
        real, imag = finish(k)
        for h, value in enumerate((real, imag)):
            at = h * cells + column[k]
            out_one[:, at : at + width] = value
            a, b = near[h], far[h]
            mask[k, c, h, a, b, z] = low(value)
            at = mask.at[k, c, h, a, b, z]
            if k == Z_FIRST:
                arrivals["g", 0, k, h] = send(at, at, far_dev[h])
            else:
                for i in range(1, depth):
                    arrivals["g", 0, k, h, i] = send(at, at, along_z[i - 1])

    def gather_far(k):
        for h in range(2):
            if k == Z_FIRST:
                arrivals["g", 0, k, h].wait_recv()
                at = mask.at[k, c, h, near[h], :, z]
                arrivals["g", 1, k, h] = send(at, at, near_dev[h])
            else:
                for i in range(1, depth):
                    arrivals["g", 0, k, h, i].wait_recv()
                at = mask.at[k, c, h, near[h], far[h]]
                arrivals["g", 1, k, h] = send(at, at, far_dev[h])

    def gather_near(k):
        for h in range(2):
            arrivals["g", 1, k, h].wait_recv()
            if k == Z_FIRST:
                at = mask.at[k, c, h, :, :, z]
                for i in range(1, depth):
                    arrivals["g", 2, k, h, i] = send(at, at, along_z[i - 1])
            else:
                at = mask.at[k, c, h, near[h]]
                arrivals["g", 2, k, h] = send(at, at, near_dev[h])

    def gather_core(k):
        for h in range(2):
            if k == Z_FIRST:
                for i in range(1, depth):
                    arrivals["g", 2, k, h, i].wait_recv()
            else:
                arrivals["g", 2, k, h].wait_recv()
        at = mask.at[k, c]
        arrivals["g", 3, k] = send(at, at, sibling)

    def gather_done(k):
        arrivals["g", 3, k].wait_recv()

        @pl.loop(0, depth)
        def _(zz):
            for cc in range(2):
                for yy in range(2):
                    for xx in range(2):
                        start = pl.multiple_of((((zz * 2 + cc) * 2 + yy) * 2 + xx) * strip, strip)
                        field = field_at(start, strip, k)
                        for h in range(2):
                            a, b = ((xx, yy), (yy, xx))[h]
                            applied[k, h, pl.ds(start, strip), :] = mask[k, cc, h, a, b, zz] * field

    def columns_part(zz, part):
        start = pl.multiple_of(zz * block, block)
        sides = [
            [applied[part * 4 + q, h, pl.ds(start, block), :] for q in range(4)] for h in range(2)
        ]
        for r, pair in enumerate(four_sums(sides[0], sides[1], -1)):
            both = jnp.concatenate(pair, axis=1)
            rows = slice(part * 2 * width, (part + 1) * 2 * width)
            out = jnp.dot(both, table_col[r, rows], preferred_element_type=jnp.float32)
            if part > 0:
                out += partial[r, pl.ds(start, block), :]
            if part < pieces - 1:
                partial[r, pl.ds(start, block), :] = out
            else:
                yield out

    def early_columns(k):
        gather_done(k)
        for zz in range(depth):
            part, last = divmod(k - zz - 3, 4)
            if last == 0 and 0 <= part < pieces - 1:
                for _ in columns_part(zz, part):
                    pass

    def schedule(stages, keys, between=None):
        order = sorted(
            (keys[s][0] + keys[s][1] * k, -s, k) for s in range(len(stages)) for k in range(chunks)
        )
        waiting, done = [(-s, k) for _, s, k in order], []
        while waiting:
            s, k = next((s, k) for s, k in waiting if s == 0 or (s - 1, k) in done)
            waiting.remove((s, k))
            done.append((s, k))
            if between and len(done) == 2 * chunks:
                between()
            stages[s](k)

    def build_tables():
        one = lax.broadcasted_iota(jnp.int32, (quarter, quarter), 0)
        two = lax.broadcasted_iota(jnp.int32, (quarter, quarter), 1)
        square = lax.rem((one - two) * (one - two), 2 * cells)
        phase = square.astype(jnp.float32) * (math.pi / cells)
        factor = cells ** (-0.5)
        real, imag = wide(low(jnp.cos(phase) * factor)), wide(low(jnp.sin(phase) * factor))
        for r in range(4):
            keep = ((two - one) & 3) == r
            rr, ii = low(jnp.where(keep, real, 0.0)), low(jnp.where(keep, imag, 0.0))
            for n in range(pieces):
                rows = slice(n * width, (n + 1) * width)
                to = 2 * n * width
                table_col[r, to : to + width, :quarter] = rr[rows]
                table_col[r, to : to + width, quarter:] = ii[rows]
                table_col[r, to + width : to + 2 * width, :quarter] = -ii[rows]
                table_col[r, to + width : to + 2 * width, quarter:] = rr[rows]
            keep = ((one - two) & 3) == r
            rr, ii = low(jnp.where(keep, real, 0.0)), low(jnp.where(keep, imag, 0.0))
            table_row[r, :quarter, :quarter] = rr
            table_row[r, quarter:, quarter:] = rr
            table_row[r, :quarter, quarter:] = -ii
            table_row[r, quarter:, :quarter] = ii

    schedule(
        (product, near_send, far_send, z_send, first_mask, gather_far, gather_near, gather_core, early_columns),
        KEYS, build_tables,
    )

    @pl.loop(0, depth)
    def _(zz):
        start = pl.multiple_of(zz * block, block)
        outs = list(columns_part(zz, pieces - 1))
        done = four_sums([o[:, :quarter] for o in outs], [o[:, quarter:] for o in outs], 1.0)
        for p in range(4):
            for h in range(2):
                spread[p, h, pl.ds(start, block), :] = low(done[p][h])

    core_send2, near_send2, far_send2, z_send2, finish2 = reduce_stages(
        2, sums2, from_core2, from_near2, from_far2, from_z2, z_first2
    )

    def arrive(k):
        if k == 0:
            loads["second"].wait()
        piece = pl.ds(k // 4 * width, width)
        sides = [
            [spread[k % 4, h, q * quarter : (q + 1) * quarter, piece] for q in range(4)]
            for h in range(2)
        ]
        outs = []
        for r, pair in enumerate(four_sums(sides[0], sides[1], -1)):
            both = jnp.concatenate(pair, axis=0)
            outs.append(jnp.dot(table_row[r], both, preferred_element_type=jnp.float32))
        done = four_sums([o[:quarter] for o in outs], [o[quarter:] for o in outs], 1.0)
        for p in range(4):
            rows = slice(p * quarter, (p + 1) * quarter)
            back_real = wide(second[rows, column[k] : column[k] + width])
            back_imag = wide(second[rows, cells + column[k] : cells + column[k] + width])
            arr_real, arr_imag = done[p]
            terms = (
                back_real * arr_real + back_imag * arr_imag,
                back_imag * arr_real - back_real * arr_imag,
            )
            for h in range(2):
                value = low(terms[h])
                for n in range(quarter // strip):
                    number = p * (quarter // strip) + n
                    xx, yy, cc, zz = number % 2, number // 2 % 2, number // 4 % 2, number // 8
                    a, b = ((xx, yy), (yy, xx))[h]
                    sums2[k, cc, h, a, b, zz] = value[n * strip : (n + 1) * strip]
        core_send2(k)

    def second_mask(k):
        real, imag = finish2(k)
        out_two[:, column[k] : column[k] + width] = real
        out_two[:, cells + column[k] : cells + column[k] + width] = imag

    schedule((arrive, near_send2, far_send2, z_send2, second_mask), KEYS_TWO)
    for copy in sent:
        copy.wait_send()


def hand_on_kernel(one_in, two_in, one_out, two_out):
    one_out[...] = one_in[...]
    two_out[...] = two_in[...]


def sweep_call(modes, back_first, back_second, devices, depth, scale):
    cells = back_first.shape[0]
    strip, width, chunks = cells // devices, cells // CHUNKS, CHUNKS
    low = jnp.bfloat16
    tail = (strip, width)
    received = [
        pltpu.VMEM((chunks, 2, 2, 2, depth) + tail, low),
        pltpu.VMEM((chunks, 2, 2, depth) + tail, low),
        pltpu.VMEM((chunks, 2, depth) + tail, low),
        pltpu.VMEM((chunks, 2, depth - 1) + tail, low),
        pltpu.VMEM((2, depth - 1, 2, 2) + tail, low),
    ]
    whole = pltpu.VMEM((chunks, 2, 2, 2, 2, depth) + tail, low)
    table = pltpu.VMEM((4, cells // 2, cells // 2), low)
    copies = 3 * chunks * 2 * (3 + depth - 1)
    vmem = pl.BlockSpec(memory_space=pltpu.VMEM)
    hbm = pl.BlockSpec(memory_space=pl.ANY)
    out = jax.ShapeDtypeStruct((strip, 2 * cells), jnp.float32)
    swept = pl.pallas_call(
        functools.partial(sweep_kernel, depth, scale),
        out_shape=(out, out),
        in_specs=[vmem, hbm, hbm],
        out_specs=(vmem, vmem),
        scratch_shapes=[pltpu.VMEM((cells, 2 * cells), low)] * 2
        + [whole] + received + [whole] + received
        + [whole] + [pltpu.VMEM((chunks, 2, cells, width), low), pltpu.VMEM((4, 2, cells, cells // 4), low)]
        + [pltpu.VMEM((4, cells, cells // 2), jnp.float32), table, table]
        + [pltpu.VMEM((cells, 128), jnp.float32), pltpu.VMEM((1, cells), jnp.float32)]
        + [
            pltpu.SemaphoreType.DMA((2 * chunks + 1,)),
            pltpu.SemaphoreType.DMA((copies,)),
            pltpu.SemaphoreType.DMA((copies,)),
        ],
        compiler_params=pltpu.CompilerParams(
            collective_id=0, has_side_effects=True, vmem_limit_bytes=60 * 1024 * 1024
        ),
        name="sweep",
    )(modes, back_first, back_second)
    return pl.pallas_call(
        hand_on_kernel,
        out_shape=(out, out),
        in_specs=[vmem, vmem],
        out_specs=(vmem, vmem),
        compiler_params=pltpu.CompilerParams(vmem_limit_bytes=63 * 1024 * 1024),
        name="hand_on",
    )(*swept)


def body(in_modes, back_first, back_second):
    mode_dev = in_modes.shape[0]
    cells = back_first.shape[1]
    axes = ("mgroup", "msub")
    devices_all = lax.axis_size("mgroup") * lax.axis_size("msub")
    scale_all = float(mode_dev * devices_all) ** (-0.5)
    depth = lax.axis_size("mgroup") // 2
    if mode_dev == 1 and lax.axis_size("msub") == 4 and depth == 4 and cells % (16 * devices_all) == cells % (128 * CHUNKS) == 0:
        return sweep_call(
            in_modes, back_first[0], back_second[0], devices_all, depth, scale_all
        )
    herm_table = hermite_table(grid_points(cells))
    row_funcs = pick_funcs(in_modes[:, 0], herm_table)
    col_funcs = pick_funcs(in_modes[:, 1], herm_table)
    fields = (row_funcs[:, :, None] * col_funcs[:, None, :]).astype(jnp.bfloat16)
    table = residue_chirp(cells)
    first = intersection_first(back_first, fields).astype(jnp.bfloat16)
    summed = lax.psum_scatter(first, axes, scatter_dimension=0, tiled=True)
    mask_first = soften(summed.astype(jnp.float32) * scale_all)
    full_mask = lax.all_gather(mask_first.astype(jnp.bfloat16), axes, axis=0, tiled=True)
    full_mask = full_mask.astype(jnp.float32)
    real_part, imag_part = 0.0, 0.0
    for mode in range(mode_dev):
        field = fields[mode].astype(jnp.float32)
        real = (full_mask[:, :cells] * field).astype(jnp.bfloat16).astype(jnp.float32)
        imag = (full_mask[:, cells:] * field).astype(jnp.bfloat16).astype(jnp.float32)
        arr_real, arr_imag = propagate_down(*propagate_columns(real, imag, table), table)
        back = back_second[mode].astype(jnp.float32)
        back_real, back_imag = back[:, :cells], back[:, cells:]
        real_part += back_real * arr_real + back_imag * arr_imag
        imag_part += back_imag * arr_real - back_real * arr_imag
    second = jnp.concatenate([real_part, imag_part], axis=1).astype(jnp.bfloat16)
    summed_two = lax.psum_scatter(second, axes, scatter_dimension=0, tiled=True)
    mask_second = soften(summed_two.astype(jnp.float32) * scale_all)
    return (mask_first, mask_second)


def solution(mesh):
    placed = (
        P(("mgroup", "msub"), None),
        P(("mgroup", "msub"), None, None),
        P(("mgroup", "msub"), None, None),
    )
    return jax.shard_map(
        body,
        mesh=mesh,
        in_specs=placed,
        out_specs=(P(("mgroup", "msub"), None), P(("mgroup", "msub"), None)),
        check_vma=False,
    )
```
